512 devices in a mesh: ctx: 128 (over z_lo, x, y), head: 2 (over z_hi), rep: 2 (over core).
Axes of the slice: x: 4, y: 8, z: 8 (z_hi: 2, z_lo: 4; z = z_hi * 4 + z_lo), core: 2. Of those that a mesh axis runs over, the one named last changes fastest.
Arguments:
- seq_values: bfloat16 [65536, 4096], P(('rep', 'ctx'), 'head'), parts along dimension 0, may hold values from -6 to 6
- seq_gate: bfloat16 [65536, 4096], P(('rep', 'ctx'), 'head'), parts along dimension 0, may hold values from -6 to 6
- seq_keys: bfloat16 [65536, 128], P(('rep', 'ctx')), parts along dimension 0, may hold values from -6 to 6
- seq_queries: bfloat16 [65536, 128], P(('rep', 'ctx')), parts along dimension 0, may hold values from -0.5 to 0.5
- level_weights: bfloat16 [16, 64, 65536], P(None, 'head', ('rep', 'ctx')), parts along dimension 2, may hold values from 0 to 4
- skip_gain: float32 [64], P('head'), may hold values from 0.5 to 2
- norm_gain: float32 [4096], P('head'), may hold values from 0.5 to 1.5
- out_weight: bfloat16 [4096, 2048], P('head', 'ctx'), may hold values from -0.09375 to 0.09375
Outputs:
- mixer_out: bfloat16 [65536, 2048], P(('rep', 'ctx'), 'head'), parts along dimension 0
The draws below stay inside these ranges and needn't reach their ends.
There are 2 independent parts, one for each index of `rep`. The reference program is written for one: setup_inputs(seed, part) draws one part's arguments, and reference() takes and returns one part's arrays. A program takes and returns all parts, laid end to end along the dimension named above; an argument that names none is the same for every part. Nothing has to cross between parts.
All inputs are finite; a program needn't handle non-finite values.
Results may differ from the reference program's by a relative error of at most 0.0054.
Values may be sent and summed in bfloat16 or wider, within the bound.
No kernel may reach another device: no remote copies, remote signals or barrier semaphores. Data moves between devices by JAX's collectives and lax.ppermute only.
A program may use at most 64 MiB of HBM per device.

```python
import math
import jax
import jax.numpy as jnp
from jax import lax

D = 2048
HEADS = 64
P_SIZE = 64
N = 128
TOK_DEV = 256
TOKENS = 32768
LEVELS = 16
N_HEAD = 2


def draw_level_weights(key, part):
    shape = (LEVELS, HEADS, TOKENS)
    depth = jnp.arange(LEVELS, dtype=jnp.float32)[:, None, None]
    damping = jnp.exp2(-0.5 * depth)
    base = jnp.exp(jax.random.uniform(key, shape, jnp.float32, math.log(0.25), math.log(4.0)))
    return (base * damping).astype(jnp.bfloat16)


def steps_of(stream_key, dims, cuts, low, high):
    def one(axis_at, parts):
        heights = jax.random.uniform(jax.random.fold_in(jax.random.fold_in(stream_key, 6), axis_at), (parts,), jnp.float32, low / len(cuts), high / len(cuts))
        return jnp.repeat(jnp.exp(heights), dims[axis_at] // parts).reshape((-1,) + (1,) * (len(dims) - axis_at - 1))

    factor_of = one(*cuts[0])
    for cut in cuts[1:]:
        factor_of = factor_of * one(*cut)
    return factor_of


def bell_draw(rng, dims, deviation, reach, cuts=(), kind=jnp.bfloat16):
    gain = steps_of(rng, dims, cuts, -0.22, 0.18) if cuts else 1.0
    values = jax.random.normal(rng, dims, jnp.float32) * deviation * gain
    return jnp.minimum(jnp.maximum(values, -reach), reach).astype(kind)


def setup_inputs(seed: int = 0, part: int = 0) -> dict:
    seeds = jax.random.split(jax.random.key(seed), 9)
    part_keys = jax.random.split(jax.random.fold_in(seeds[8], part), 9)
    return {
        "seq_values": bell_draw(part_keys[0], (TOKENS, HEADS * P_SIZE), 1.0, 6.0, ((0, 128), (1, 2))),
        "seq_gate": bell_draw(part_keys[1], (TOKENS, HEADS * P_SIZE), 1.0, 6.0, ((0, 128), (1, 2))),
        "seq_keys": bell_draw(part_keys[2], (TOKENS, N), 1.0, 6.0, ((0, 128),)),
        "seq_queries": bell_draw(part_keys[3], (TOKENS, N), N ** -0.5, 0.5, ((0, 128),)),
        "level_weights": draw_level_weights(jax.random.fold_in(jax.random.fold_in(seeds[8], part), 71), part),
        "skip_gain": jnp.clip(0.5 + 1.5 * jax.random.uniform(seeds[5], (HEADS,), jnp.float32) ** steps_of(seeds[5], (HEADS,), ((0, 2),), -0.2, 0.2), 0.5, 2.0),
        "norm_gain": jnp.clip(1.0 + 0.1 * jax.random.normal(seeds[6], (HEADS * P_SIZE,), jnp.float32), 0.5, 1.5),
        "out_weight": bell_draw(seeds[7], (HEADS * P_SIZE, D), (HEADS * P_SIZE) ** -0.5, 0.09375, ((0, 2), (1, 128))),
    }


epsilon = 1e-05

def bit_span(differ, count):
    level_of = jnp.zeros_like(differ)
    for level_bit in range(count):
        level_of = level_of + (jnp.right_shift(differ, level_bit) > 0).astype(jnp.int32)
    return level_of

def reference(seq_values, seq_gate, seq_keys, seq_queries, level_weights, skip_gain, norm_gain, out_weight):
    tok_rows = TOK_DEV
    blocks = TOKENS // tok_rows
    local_bits = tok_rows.bit_length() - 1
    far_levels = blocks.bit_length() - 1
    width = HEADS * P_SIZE
    weights = level_weights.astype(jnp.float32)
    value_blocks = seq_values.reshape(blocks, tok_rows, width)
    key_blocks = seq_keys.reshape(blocks, tok_rows, N)

    def block_state(pieces):
        return jnp.dot(pieces[0].T, pieces[1], preferred_element_type=jnp.float32)
    states = lax.map(block_state, (key_blocks, value_blocks))
    pyramid = [states]
    for level_bit in range(far_levels - 1):
        pyramid.append(pyramid[-1].reshape(-1, 2, N, width).sum(axis=1))
    places = jnp.arange(tok_rows, dtype=jnp.int32)
    differ = jnp.bitwise_xor(places[:, None], places[None, :])
    level_of = bit_span(differ, local_bits)
    causal = places[None, :] <= places[:, None]
    onehot = ((level_of[None] == jnp.arange(local_bits + 1, dtype=jnp.int32)[:, None, None]) & causal[None]).astype(jnp.float32)

    def one_block(block_id):
        offset = block_id * tok_rows
        values_b = lax.dynamic_slice_in_dim(seq_values, offset, tok_rows, 0)
        gate_b = lax.dynamic_slice_in_dim(seq_gate, offset, tok_rows, 0)
        keys_b = lax.dynamic_slice_in_dim(seq_keys, offset, tok_rows, 0)
        query_b = lax.dynamic_slice_in_dim(seq_queries, offset, tok_rows, 0)
        weight_b = lax.dynamic_slice_in_dim(weights, offset, tok_rows, 2)
        mixing = jnp.einsum('lht,lts->hts', weight_b[:local_bits + 1], onehot, precision=lax.Precision.HIGHEST)
        scores = jnp.dot(query_b, keys_b.T, preferred_element_type=jnp.float32)
        weighted = (mixing * scores[None]).astype(jnp.bfloat16)
        values = values_b.astype(jnp.float32).reshape(tok_rows, HEADS, P_SIZE)
        mixed = jnp.einsum('hts,shp->thp', weighted.astype(jnp.float32), values, precision=lax.Precision.HIGHEST)
        mixed = mixed + skip_gain[None, :, None] * values
        query_f32 = query_b.astype(jnp.float32)
        for level_bit in range(far_levels):
            group_id = jnp.right_shift(block_id, level_bit)
            is_upper = jnp.bitwise_and(group_id, 1).astype(jnp.float32)
            sibling = lax.dynamic_index_in_dim(pyramid[level_bit], jnp.maximum(group_id - 1, 0).astype(jnp.int32), 0, keepdims=False)
            readout = jnp.dot(query_f32, sibling, precision=lax.Precision.HIGHEST).reshape(tok_rows, HEADS, P_SIZE)
            scale_t = weight_b[local_bits + 1 + level_bit].T * is_upper
            mixed = mixed + scale_t[:, :, None] * readout
        gated = mixed.reshape(tok_rows, width) * jax.nn.silu(gate_b.astype(jnp.float32))
        grouped = gated.reshape(tok_rows, N_HEAD, width // N_HEAD)
        mean_sq = lax.optimization_barrier(jnp.mean(grouped * grouped, axis=2, keepdims=True))
        normed = (grouped * lax.rsqrt(mean_sq + epsilon)).reshape(tok_rows, width) * norm_gain[None, :]
        normed = normed.astype(jnp.bfloat16)
        return jnp.dot(normed, out_weight, preferred_element_type=jnp.float32).astype(jnp.bfloat16)
    result = lax.map(one_block, jnp.arange(blocks, dtype=jnp.int32))
    return result.reshape(TOKENS, D)
```

```python
import functools

import jax
import jax.numpy as jnp
from jax import lax
from jax.experimental import pallas as pl
from jax.experimental.pallas import tpu as pltpu
from jax.sharding import Mesh, PartitionSpec as P

epsilon = 1e-05
LOCAL_LEVELS = 9
NN = (((1,), (0,)), ((), ()))
NT = (((1,), (1,)), ((), ()))
f32 = jnp.float32
bf16 = jnp.bfloat16


def params(mib, steps=1):
    return pltpu.CompilerParams(
        vmem_limit_bytes=mib * 2**20, dimension_semantics=("arbitrary",) * steps
    )


def cost(flops, moved):
    return pl.CostEstimate(flops=flops, bytes_accessed=moved, transcendentals=0)


def swapped(value, axis, mask):
    return lax.ppermute(value, axis, [(i, i ^ mask) for i in range(lax.axis_size(axis))])


def dot(a, b, dims):
    return lax.dot_general(a, b, dims, preferred_element_type=f32)


def state_kernel(values_ref, keys_ref, vt_ref, st_ref, sb_ref):
    vt = values_ref[...].T
    vt_ref[...] = vt
    st = dot(vt, keys_ref[...], NN)
    st_ref[...] = st
    sb_ref[...] = st.astype(bf16)


def own_state(values, keys, chunk, chunks):
    tok, width = values.shape
    cols = width // chunks
    n = keys.shape[1]
    return pl.pallas_call(
        state_kernel,
        grid=(1,),
        in_specs=[
            pl.BlockSpec((tok, cols), lambda i: (0, chunk)),
            pl.BlockSpec((tok, n), lambda i: (0, 0)),
        ],
        out_specs=[
            pl.BlockSpec((cols, tok), lambda i: (0, 0)),
            pl.BlockSpec((cols, n), lambda i: (0, 0)),
            pl.BlockSpec((cols, n), lambda i: (0, 0)),
        ],
        out_shape=[
            jax.ShapeDtypeStruct((cols, tok), bf16),
            jax.ShapeDtypeStruct((cols, n), f32),
            jax.ShapeDtypeStruct((cols, n), bf16),
        ],
        compiler_params=params(24),
        cost_estimate=cost(2 * tok * cols * n, 4 * tok * cols),
        name="own_state",
    )(values, keys)


def local_kernel(heads, half, skip_ref, vt_ref, gate_ref, keys_ref, query_ref, w_ref, acc_ref, silu_ref, score_ref):
    size = vt_ref.shape[0] // heads
    first = pl.program_id(0) * heads

    @pl.when(pl.program_id(0) == 0)
    def _():
        scores = dot(keys_ref[...], query_ref[...], NT)
        s = lax.broadcasted_iota(jnp.int32, scores.shape, 0)
        t = lax.broadcasted_iota(jnp.int32, scores.shape, 1)
        score_ref[...] = jnp.where(s <= t, scores, 0.0)

    gate = gate_ref[...].astype(f32)
    silu_ref[...] = (gate / (1.0 + jnp.exp(-gate))).T

    s = lax.broadcasted_iota(jnp.int32, (half, half), 0)
    t = lax.broadcasted_iota(jnp.int32, (half, half), 1)
    differ = s ^ t
    low = score_ref[:half, :half]
    cross = score_ref[:half, half:]
    high = score_ref[half:, half:]
    for h in range(heads):
        w = w_ref[:, h, :].astype(f32)

        def mix(level, lo):
            return jnp.broadcast_to(w[level : level + 1, lo : lo + half], (half, half))

        def diagonal(lo, scores):
            m = mix(0, lo)
            for level in range(1, LOCAL_LEVELS - 1):
                m = jnp.where(differ >= (1 << (level - 1)), mix(level, lo), m)
            return (m * scores).astype(bf16)

        vt = vt_ref[h * size : (h + 1) * size, :]
        skip = skip_ref[first + h]
        near = dot(vt[:, :half], diagonal(0, low), NN)
        right = jnp.concatenate(
            [(mix(LOCAL_LEVELS - 1, half) * cross).astype(bf16), diagonal(half, high)], axis=0
        )
        far = dot(vt, right, NN)
        rows = slice(h * size, (h + 1) * size)
        acc_ref[rows, :half] = near + skip * vt[:, :half].astype(f32)
        acc_ref[rows, half:] = far + skip * vt[:, half:].astype(f32)


def local_part(vt, gate, keys, query, weights, skip, chunk, head_size):
    cols, tok = vt.shape
    n = keys.shape[1]
    heads = 8
    rows = heads * head_size
    steps = cols // rows
    return pl.pallas_call(
        functools.partial(local_kernel, heads, tok // 2),
        grid=(steps,),
        in_specs=[
            pl.BlockSpec(memory_space=pltpu.SMEM),
            pl.BlockSpec((rows, tok), lambda i: (i, 0)),
            pl.BlockSpec((tok, rows), lambda i: (0, chunk * steps + i)),
            pl.BlockSpec((tok, n), lambda i: (0, 0)),
            pl.BlockSpec((tok, n), lambda i: (0, 0)),
            pl.BlockSpec((16, heads, tok), lambda i: (0, chunk * steps + i, 0)),
        ],
        out_specs=[
            pl.BlockSpec((rows, tok), lambda i: (i, 0)),
            pl.BlockSpec((rows, tok), lambda i: (i, 0)),
        ],
        out_shape=[jax.ShapeDtypeStruct((cols, tok), f32)] * 2,
        scratch_shapes=[pltpu.VMEM((tok, tok), f32)],
        compiler_params=params(24),
        cost_estimate=cost(8 * tok * tok * cols, 12 * tok * cols),
        name="local_part",
    )(skip[chunk * steps * heads : (chunk + 1) * steps * heads], vt, gate, keys, query, weights)


def read_levels(acc, states, weights, query):
    heads = weights.shape[1]
    rows, tok = acc.shape
    size = rows // heads
    for level, state in enumerate(states):
        part = dot(state, query, NT).reshape(heads, size, tok)
        acc = acc + (part * weights[level][:, None, :]).reshape(rows, tok)
    return acc


def far_kernel(count, *refs):
    states = [ref[...] for ref in refs[:count]]
    acc_ref, query_ref, w_ref, out_ref = refs[count:]
    out_ref[...] = read_levels(acc_ref[...], states, w_ref[...].astype(f32), query_ref[...])


def far_part(acc, states, weights, query, head_size):
    cols, tok = acc.shape
    n = query.shape[1]
    heads = 8
    rows = heads * head_size
    count = len(states)
    return pl.pallas_call(
        functools.partial(far_kernel, count),
        grid=(cols // rows,),
        in_specs=[pl.BlockSpec((rows, n), lambda i: (i, 0))] * count
        + [
            pl.BlockSpec((rows, tok), lambda i: (i, 0)),
            pl.BlockSpec((tok, n), lambda i: (0, 0)),
            pl.BlockSpec((count, heads, tok), lambda i: (0, i, 0)),
        ],
        out_specs=pl.BlockSpec((rows, tok), lambda i: (i, 0)),
        out_shape=jax.ShapeDtypeStruct((cols, tok), f32),
        compiler_params=params(24),
        cost_estimate=cost(2 * count * cols * n * tok, 8 * cols * tok),
        name="far_part",
    )(*states, acc, query, weights)


def project(where_ref, pieces, normed_ref, out_ref):
    mine = where_ref[1]
    half = normed_ref.shape[1]
    width = pieces[0].shape[1]
    for k in range(len(pieces) // 2):
        block = dot(pieces[2 * k][0], normed_ref[mine], NN)
        block = block + dot(pieces[2 * k + 1][0], normed_ref[1 - mine], NN)
        at = pl.multiple_of((where_ref[0] ^ k) * width, width)
        out_ref[:, pl.ds(at, width)] = block.T.astype(out_ref.dtype)


def finish_kernel(where_ref, *refs):
    pieces = refs[:8]
    acc_refs, silu_refs, state_refs = refs[8:10], refs[10:12], refs[12:14]
    w_ref, query_ref, gain_ref = refs[14:17]
    out_ref, normed_ref = refs[17:19]

    @pl.when(pl.program_id(0) == 0)
    def _():
        rows, tok = acc_refs[0].shape
        heads = w_ref.shape[1] // 2
        squares = jnp.zeros((1, tok), f32)
        gated = []
        for c in range(2):
            w = w_ref[:, c * heads : (c + 1) * heads, :].astype(f32)
            mixed = read_levels(acc_refs[c][...], [state_refs[c][...]], w, query_ref[...])
            part = mixed * silu_refs[c][...]
            squares = squares + jnp.sum(part * part, axis=0, keepdims=True)
            gated.append(part)
        scale = lax.rsqrt(squares / (2 * rows) + epsilon)
        for c in range(2):
            gain = gain_ref[c * rows : (c + 1) * rows, :]
            normed_ref[c] = (gated[c] * scale * gain).astype(bf16)

    project(where_ref, pieces, normed_ref, out_ref)


def keep_kernel(where_ref, *refs):
    project(where_ref, refs[:8], refs[8], refs[9])


def piece_specs(pieces, offset):
    _, cols, depth = pieces[0].shape
    return [
        pl.BlockSpec((1, cols, depth), lambda i, where: (where[offset] + i, 0, 0)) for _ in pieces
    ]


def finish(where, pieces, accs, silus, states, weights, query, gain):
    rows, tok = accs[0].shape
    z_size, cols, depth = pieces[0].shape
    steps = z_size // 2
    wide = cols * len(pieces) // 2

    def whole(array):
        return pl.BlockSpec(array.shape, lambda i, where: (0,) * array.ndim)

    others = [*accs, *silus, *states, weights, query, gain]
    return pl.pallas_call(
        finish_kernel,
        grid_spec=pltpu.PrefetchScalarGridSpec(
            num_scalar_prefetch=1,
            grid=(steps,),
            in_specs=piece_specs(pieces, 2) + [whole(a) for a in others],
            out_specs=[
                pl.BlockSpec((tok, wide), lambda i, where: (0, i)),
                pl.BlockSpec((2, rows, tok), lambda i, where: (0, 0, 0)),
            ],
        ),
        out_shape=[
            jax.ShapeDtypeStruct((tok, wide * steps), bf16),
            jax.ShapeDtypeStruct((2, rows, tok), bf16),
        ],
        compiler_params=params(40),
        cost_estimate=cost(2 * tok * 2 * rows * wide * steps, 16 * 2**20),
        name="finish",
    )(where, *pieces, *others)


def keep(where, pieces, normed):
    _, rows, tok = normed.shape
    z_size, cols, depth = pieces[0].shape
    steps = z_size // 2
    wide = cols * len(pieces) // 2
    return pl.pallas_call(
        keep_kernel,
        grid_spec=pltpu.PrefetchScalarGridSpec(
            num_scalar_prefetch=1,
            grid=(steps,),
            in_specs=piece_specs(pieces, 3)
            + [pl.BlockSpec((2, rows, tok), lambda i, where: (0, 0, 0))],
            out_specs=pl.BlockSpec((tok, wide), lambda i, where: (0, i)),
        ),
        out_shape=jax.ShapeDtypeStruct((tok, wide * steps), f32),
        compiler_params=params(40),
        cost_estimate=cost(2 * tok * 2 * rows * wide * steps, 8 * 2**20),
        name="keep",
    )(where, *pieces, normed)


def gathered_weight(out_weight):
    z_size, y_size = lax.axis_size("zl"), lax.axis_size("y")
    rows, cols = out_weight.shape
    mine = lax.axis_index("rep")
    half = lax.dynamic_slice_in_dim(out_weight, mine * (rows // 2), rows // 2, 0).T
    spread = jnp.broadcast_to(half[None], (z_size * y_size, cols, rows // 2))
    got = lax.all_to_all(spread, ("zl", "y"), 0, 0, tiled=True)
    own = got.reshape(z_size, y_size * cols, rows // 2)
    pieces = []
    for k in range(lax.axis_size("x")):
        piece = own if k == 0 else swapped(own, "x", k)
        pieces += [piece, swapped(piece, "rep", 1)]
    return pieces


def on_device(
    seq_values, seq_gate, seq_keys, seq_queries, level_weights, skip_gain, norm_gain, out_weight
):
    width = seq_values.shape[1]
    head_count = skip_gain.shape[0]
    head_size = width // head_count
    chunks = 2
    chunk_heads = head_count // chunks
    axes = [("y", b) for b in range(3)] + [("x", b) for b in range(2)] + [("zl", b) for b in range(2)]
    uppers = jnp.stack([(lax.axis_index(a) >> b) & 1 for a, b in axes])
    far_weights = level_weights[LOCAL_LEVELS:] * uppers[:, None, None].astype(bf16)

    pieces = gathered_weight(out_weight)

    accs, silus, tops = [], [], []
    for c in range(chunks):
        vt, state, sent = own_state(seq_values, seq_keys, c, chunks)
        acc, silu = local_part(vt, seq_gate, seq_keys, seq_queries, level_weights, skip_gain, c, head_size)
        received = []
        for axis, bit in axes[:-1]:
            got = swapped(sent, axis, 1 << bit)
            received.append(got)
            state = state + got.astype(f32)
            sent = state.astype(bf16)
        axis, bit = axes[-1]
        step = 1 << bit
        top = lax.ppermute(sent, axis, [(i, i + step) for i in range(lax.axis_size(axis) - step)])
        heads = slice(c * chunk_heads, (c + 1) * chunk_heads)
        acc = far_part(acc, received[:3], far_weights[:3, heads], seq_queries, head_size)
        acc = far_part(acc, received[3:], far_weights[3:6, heads], seq_queries, head_size)
        accs.append(acc)
        silus.append(silu)
        tops.append(top)

    head = lax.axis_index("head")
    z_half = lax.axis_size("zl") // 2
    where = jnp.stack(
        [lax.axis_index("x"), lax.axis_index("rep"), (1 - head) * z_half, head * z_half]
    ).astype(jnp.int32)
    to_send, normed = finish(
        where, pieces, accs, silus, tops, far_weights[6:], seq_queries, norm_gain[:, None]
    )
    got = swapped(to_send, "head", 1)
    kept = keep(where, pieces, normed)
    return (kept + got.astype(f32)).astype(bf16)


def solution(mesh):
    grid = Mesh(mesh.devices.reshape(4, 4, 8, 2, 2), ("zl", "x", "y", "head", "rep"))
    ctx = ("zl", "x", "y")
    tokens = ("rep", *ctx)
    placed = (
        P(tokens, "head"),
        P(tokens, "head"),
        P(tokens, None),
        P(tokens, None),
        P(None, "head", tokens),
        P("head"),
        P("head"),
        P("head", ctx),
    )
    return jax.shard_map(
        on_device, mesh=grid, in_specs=placed, out_specs=P(tokens, "head"), check_vma=False
    )
```

```python
import functools

import jax
import jax.numpy as jnp
from jax import lax
from jax.experimental import pallas as pl
from jax.experimental.pallas import tpu as pltpu
from jax.sharding import Mesh, PartitionSpec as P

epsilon = 1e-05
LOCAL_LEVELS = 9
NN = (((1,), (0,)), ((), ()))
NT = (((1,), (1,)), ((), ()))
f32 = jnp.float32
bf16 = jnp.bfloat16


def params(mib, steps=1):
    return pltpu.CompilerParams(
        vmem_limit_bytes=mib * 2**20, dimension_semantics=("arbitrary",) * steps
    )


def cost(flops, moved):
    return pl.CostEstimate(flops=flops, bytes_accessed=moved, transcendentals=0)


def swapped(value, axis, mask):
    return lax.ppermute(value, axis, [(i, i ^ mask) for i in range(lax.axis_size(axis))])


def dot(a, b, dims):
    return lax.dot_general(a, b, dims, preferred_element_type=f32)


def state_kernel(values_ref, keys_ref, vt_ref, sent_ref):
    vt = values_ref[...].T
    vt_ref[...] = vt
    sent_ref[...] = dot(vt, keys_ref[...], NN).astype(bf16)


def own_state(values, keys):
    tok, width = values.shape
    cols = width // 4
    n = keys.shape[1]
    return pl.pallas_call(
        state_kernel,
        grid=(4,),
        in_specs=[
            pl.BlockSpec((tok, cols), lambda i: (0, i)),
            pl.BlockSpec((tok, n), lambda i: (0, 0)),
        ],
        out_specs=[
            pl.BlockSpec((cols, tok), lambda i: (i, 0)),
            pl.BlockSpec((cols, n), lambda i: (i, 0)),
        ],
        out_shape=[
            jax.ShapeDtypeStruct((width, tok), bf16),
            jax.ShapeDtypeStruct((width, n), bf16),
        ],
        compiler_params=params(24),
        cost_estimate=cost(2 * tok * width * n, 4 * tok * width),
        name="own_state",
    )(values, keys)


def local_kernel(heads, half, skip_ref, vt_ref, gate_ref, keys_ref, query_ref, w_ref, acc_ref, silu_ref, score_ref):
    size = vt_ref.shape[0] // heads
    first = pl.program_id(0) * heads

    @pl.when(pl.program_id(0) == 0)
    def _():
        scores = dot(keys_ref[...], query_ref[...], NT)
        s = lax.broadcasted_iota(jnp.int32, scores.shape, 0)
        t = lax.broadcasted_iota(jnp.int32, scores.shape, 1)
        score_ref[...] = jnp.where(s <= t, scores, 0.0)

    gate = gate_ref[...].astype(f32)
    silu_ref[...] = (gate / (1.0 + jnp.exp(-gate))).T

    s = lax.broadcasted_iota(jnp.int32, (half, half), 0)
    t = lax.broadcasted_iota(jnp.int32, (half, half), 1)
    differ = s ^ t
    low = score_ref[:half, :half]
    cross = score_ref[:half, half:]
    high = score_ref[half:, half:]
    for h in range(heads):
        w = w_ref[:, h, :].astype(f32)

        def mix(level, lo):
            return jnp.broadcast_to(w[level : level + 1, lo : lo + half], (half, half))

        def diagonal(lo, scores):
            m = mix(0, lo)
            for level in range(1, LOCAL_LEVELS - 1):
                m = jnp.where(differ >= (1 << (level - 1)), mix(level, lo), m)
            return (m * scores).astype(bf16)

        vt = vt_ref[h * size : (h + 1) * size, :]
        skip = skip_ref[first + h]
        near = dot(vt[:, :half], diagonal(0, low), NN)
        right = jnp.concatenate(
            [(mix(LOCAL_LEVELS - 1, half) * cross).astype(bf16), diagonal(half, high)], axis=0
        )
        far = dot(vt, right, NN)
        rows = slice(h * size, (h + 1) * size)
        acc_ref[rows, :half] = near + skip * vt[:, :half].astype(f32)
        acc_ref[rows, half:] = far + skip * vt[:, half:].astype(f32)


def local_part(vt, gate, keys, query, weights, skip, head_size):
    cols, tok = vt.shape
    n = keys.shape[1]
    heads = 8
    rows = heads * head_size
    steps = cols // rows
    return pl.pallas_call(
        functools.partial(local_kernel, heads, tok // 2),
        grid=(steps,),
        in_specs=[
            pl.BlockSpec(memory_space=pltpu.SMEM),
            pl.BlockSpec((rows, tok), lambda i: (i, 0)),
            pl.BlockSpec((tok, rows), lambda i: (0, i)),
            pl.BlockSpec((tok, n), lambda i: (0, 0)),
            pl.BlockSpec((tok, n), lambda i: (0, 0)),
            pl.BlockSpec((16, heads, tok), lambda i: (0, i, 0)),
        ],
        out_specs=[
            pl.BlockSpec((rows, tok), lambda i: (i, 0)),
            pl.BlockSpec((rows, tok), lambda i: (i, 0)),
        ],
        out_shape=[jax.ShapeDtypeStruct((cols, tok), f32)] * 2,
        scratch_shapes=[pltpu.VMEM((tok, tok), f32)],
        compiler_params=params(24),
        cost_estimate=cost(8 * tok * tok * cols, 12 * tok * cols),
        name="local_part",
    )(skip, vt, gate, keys, query, weights)


def read_level(state, message, level, heads, n):
    rows, tok = state.shape[0], message.shape[1]
    part = dot(state, message[:n], NN).reshape(heads, rows // heads, tok)
    first = n + level * heads
    return (part * message[first : first + heads].astype(f32)[:, None, :]).reshape(rows, tok)


def sibling_sum(ref, index, bit):
    count = 1 << bit
    first = ((index >> bit) ^ 1) << bit
    if count == 1:
        return ref[first]
    total = ref[first].astype(f32)
    for k in range(1, count):
        total = total + ref[first + k].astype(f32)
    return total.astype(bf16)


def low_kernel(heads, where_ref, raw_ref, line_ref, message_ref, out_ref):
    n = raw_ref.shape[2]
    group = raw_ref.shape[0]
    local = {}
    for bit in range(3):
        for block in range(0, group, 2 << bit):
            local[bit, block] = sibling_sum(raw_ref, block + (1 << bit), bit)
    shared = [sibling_sum(line_ref, where_ref[0], bit) for bit in range(2)]
    for j in range(group):
        message = message_ref[j]
        total = read_level(shared[0], message, 3, heads, n)
        total = total + read_level(shared[1], message, 4, heads, n)
        for bit in range(3):
            if j >> bit & 1:
                block = j >> (bit + 1) << (bit + 1)
                total = total + read_level(local[bit, block], message, bit, heads, n)
        out_ref[j] = total


def high_kernel(heads, where_ref, part_ref, plane_ref, message_ref, out_ref):
    n = plane_ref.shape[2]
    shared = [sibling_sum(plane_ref, where_ref[1], bit) for bit in range(2)]
    for j in range(part_ref.shape[0]):
        message = message_ref[j]
        total = part_ref[j] + read_level(shared[0], message, 5, heads, n)
        total = total + read_level(shared[1], message, 6, heads, n)
        out_ref[j] = total.astype(bf16)


def far_call(kernel, name, heads, where, first, states, message, dtype):
    group, _, tok = message.shape
    rows = states.shape[1]
    vmem = pl.BlockSpec(memory_space=pltpu.VMEM)
    return pl.pallas_call(
        functools.partial(kernel, heads),
        in_specs=[pl.BlockSpec(memory_space=pltpu.SMEM), vmem, vmem, vmem],
        out_specs=vmem,
        out_shape=jax.ShapeDtypeStruct((group, rows, tok), dtype),
        compiler_params=pltpu.CompilerParams(vmem_limit_bytes=24 * 2**20),
        cost_estimate=cost(8 * group * rows * tok * 128, 8 * group * rows * tok),
        name=name,
    )(where, first, states, message)


def project(where_ref, pieces, normed_ref, out_ref):
    mine = where_ref[1]
    half = normed_ref.shape[1]
    width = pieces[0].shape[1]
    for k in range(len(pieces) // 2):
        block = dot(pieces[2 * k][0], normed_ref[mine], NN)
        block = block + dot(pieces[2 * k + 1][0], normed_ref[1 - mine], NN)
        at = pl.multiple_of((where_ref[0] ^ k) * width, width)
        out_ref[:, pl.ds(at, width)] = block.T.astype(out_ref.dtype)


def finish_kernel(where_ref, *refs):
    pieces = refs[:8]
    acc_ref, silu_ref, far_ref, gain_ref, out_ref, normed_ref = refs[8:]

    @pl.when(pl.program_id(0) == 0)
    def _():
        rows = acc_ref.shape[0]
        gated = (acc_ref[...] + far_ref[...].astype(f32)) * silu_ref[...]
        squares = jnp.sum(gated * gated, axis=0, keepdims=True)
        scale = lax.rsqrt(squares / rows + epsilon)
        normed = (gated * scale * gain_ref[...]).astype(bf16)
        normed_ref[0] = normed[: rows // 2]
        normed_ref[1] = normed[rows // 2 :]

    project(where_ref, pieces, normed_ref, out_ref)


def keep_kernel(where_ref, *refs):
    project(where_ref, refs[:8], refs[8], refs[9])


def piece_specs(pieces, offset):
    _, cols, depth = pieces[0].shape
    return [
        pl.BlockSpec((1, cols, depth), lambda i, where: (where[offset] + i, 0, 0)) for _ in pieces
    ]


def finish(where, pieces, acc, silu, far, gain):
    rows, tok = acc.shape
    z_size, cols, depth = pieces[0].shape
    steps = z_size // 2
    wide = cols * len(pieces) // 2

    def whole(array):
        return pl.BlockSpec(array.shape, lambda i, where: (0,) * array.ndim)

    others = [acc, silu, far, gain]
    return pl.pallas_call(
        finish_kernel,
        grid_spec=pltpu.PrefetchScalarGridSpec(
            num_scalar_prefetch=1,
            grid=(steps,),
            in_specs=piece_specs(pieces, 2) + [whole(a) for a in others],
            out_specs=[
                pl.BlockSpec((tok, wide), lambda i, where: (0, i)),
                pl.BlockSpec((2, rows // 2, tok), lambda i, where: (0, 0, 0)),
            ],
        ),
        out_shape=[
            jax.ShapeDtypeStruct((tok, wide * steps), bf16),
            jax.ShapeDtypeStruct((2, rows // 2, tok), bf16),
        ],
        compiler_params=params(40),
        cost_estimate=cost(2 * tok * rows * wide * steps, 16 * 2**20),
        name="finish",
    )(where, *pieces, *others)


def keep(where, pieces, normed):
    _, rows, tok = normed.shape
    z_size, cols, depth = pieces[0].shape
    steps = z_size // 2
    wide = cols * len(pieces) // 2
    return pl.pallas_call(
        keep_kernel,
        grid_spec=pltpu.PrefetchScalarGridSpec(
            num_scalar_prefetch=1,
            grid=(steps,),
            in_specs=piece_specs(pieces, 3)
            + [pl.BlockSpec((2, rows, tok), lambda i, where: (0, 0, 0))],
            out_specs=pl.BlockSpec((tok, wide), lambda i, where: (0, i)),
        ),
        out_shape=jax.ShapeDtypeStruct((tok, wide * steps), f32),
        compiler_params=params(40),
        cost_estimate=cost(2 * tok * 2 * rows * wide * steps, 8 * 2**20),
        name="keep",
    )(where, *pieces, normed)


def shared_along(value, axis):
    spread = jnp.broadcast_to(value[None], (lax.axis_size(axis), *value.shape))
    return lax.all_to_all(spread, axis, 0, 0, tiled=True)


def gathered_weight(out_weight):
    rows, cols = out_weight.shape
    mine = lax.axis_index("rep")
    half = lax.dynamic_slice_in_dim(out_weight, mine * (rows // 2), rows // 2, 0).T
    line = shared_along(half, "y").reshape(-1, rows // 2)
    own = shared_along(line, "zl")
    pieces = []
    for k in range(lax.axis_size("x")):
        piece = own if k == 0 else swapped(own, "x", k)
        pieces += [piece, swapped(piece, "rep", 1)]
    return pieces


def on_device(
    seq_values, seq_gate, seq_keys, seq_queries, level_weights, skip_gain, norm_gain, out_weight
):
    tok, width = seq_values.shape
    n = seq_keys.shape[1]
    head_count = skip_gain.shape[0]
    head_size = width // head_count
    group = lax.axis_size("y")
    heads = head_count // group
    rows = width // group
    axes = [("y", b) for b in range(3)] + [("x", b) for b in range(2)] + [("zl", b) for b in range(2)]
    uppers = jnp.stack([(lax.axis_index(a) >> b) & 1 for a, b in axes])
    head = lax.axis_index("head")
    z_half = lax.axis_size("zl") // 2
    place = jnp.stack([lax.axis_index("x"), lax.axis_index("zl")]).astype(jnp.int32)
    where = jnp.stack(
        [lax.axis_index("x"), lax.axis_index("rep"), (1 - head) * z_half, head * z_half]
    ).astype(jnp.int32)

    vt, sent = own_state(seq_values, seq_keys)
    raw = lax.all_to_all(sent.reshape(group, rows, n), "y", 0, 0, tiled=True)
    pieces = gathered_weight(out_weight)

    far_weights = level_weights[LOCAL_LEVELS:] * uppers[:, None, None].astype(bf16)
    levels = len(axes)
    far_weights = far_weights.reshape(levels, group, heads, tok).swapaxes(0, 1)
    far_weights = far_weights.reshape(group, levels * heads, tok)
    far_weights = jnp.pad(far_weights, ((0, 0), (0, -levels * heads % 16), (0, 0)))
    message = jnp.concatenate(
        [jnp.broadcast_to(seq_queries.T[None], (group, n, tok)), far_weights], axis=1
    )
    message = lax.all_to_all(message, "y", 0, 0, tiled=True)

    def summed(blocks):
        return jnp.sum(blocks.astype(f32), axis=0).astype(bf16)

    line = shared_along(summed(raw), "x")
    plane = shared_along(summed(line), "zl")

    acc, silu = local_part(vt, seq_gate, seq_keys, seq_queries, level_weights, skip_gain, head_size)
    part = far_call(low_kernel, "low_levels", heads, place, raw, line, message, f32)
    far = far_call(high_kernel, "high_levels", heads, place, part, plane, message, bf16)
    far = lax.all_to_all(far, "y", 0, 0, tiled=True).reshape(width, tok)

    to_send, normed = finish(where, pieces, acc, silu, far, norm_gain[:, None])
    got = swapped(to_send, "head", 1)
    kept = keep(where, pieces, normed)
    return (kept + got.astype(f32)).astype(bf16)


def solution(mesh):
    grid = Mesh(mesh.devices.reshape(4, 4, 8, 2, 2), ("zl", "x", "y", "head", "rep"))
    ctx = ("zl", "x", "y")
    tokens = ("rep", *ctx)
    placed = (
        P(tokens, "head"),
        P(tokens, "head"),
        P(tokens, None),
        P(tokens, None),
        P(None, "head", tokens),
        P("head"),
        P("head"),
        P("head", ctx),
    )
    return jax.shard_map(
        on_device, mesh=grid, in_specs=placed, out_specs=P(tokens, "head"), check_vma=False
    )
```

```python
import functools

import jax
import jax.numpy as jnp
from jax import lax
from jax.experimental import pallas as pl
from jax.experimental.pallas import tpu as pltpu
from jax.sharding import Mesh, PartitionSpec as P

epsilon = 1e-05
LOCAL_LEVELS = 9
NN = (((1,), (0,)), ((), ()))
NT = (((1,), (1,)), ((), ()))
f32 = jnp.float32
bf16 = jnp.bfloat16


def params(mib, steps=1):
    return pltpu.CompilerParams(
        vmem_limit_bytes=mib * 2**20, dimension_semantics=("arbitrary",) * steps
    )


def cost(flops, moved):
    return pl.CostEstimate(flops=flops, bytes_accessed=moved, transcendentals=0)


def swapped(value, axis, mask):
    return lax.ppermute(value, axis, [(i, i ^ mask) for i in range(lax.axis_size(axis))])


def dot(a, b, dims):
    return lax.dot_general(a, b, dims, preferred_element_type=f32)


def state_kernel(values_ref, keys_ref, vt_ref, sent_ref):
    vt = values_ref[...].T
    vt_ref[...] = vt
    sent_ref[...] = dot(vt, keys_ref[...], NN).astype(bf16)


def own_state(values, keys):
    tok, width = values.shape
    cols = width // 4
    n = keys.shape[1]
    return pl.pallas_call(
        state_kernel,
        grid=(4,),
        in_specs=[
            pl.BlockSpec((tok, cols), lambda i: (0, i)),
            pl.BlockSpec((tok, n), lambda i: (0, 0)),
        ],
        out_specs=[
            pl.BlockSpec((cols, tok), lambda i: (i, 0)),
            pl.BlockSpec((cols, n), lambda i: (i, 0)),
        ],
        out_shape=[
            jax.ShapeDtypeStruct((width, tok), bf16),
            jax.ShapeDtypeStruct((width, n), bf16),
        ],
        compiler_params=params(24),
        cost_estimate=cost(2 * tok * width * n, 4 * tok * width),
        name="own_state",
    )(values, keys)


def local_kernel(heads, half, skip_ref, vt_ref, gate_ref, keys_ref, query_ref, w_ref, acc_ref, silu_ref, score_ref):
    size = vt_ref.shape[0] // heads
    first = pl.program_id(0) * heads

    @pl.when(pl.program_id(0) == 0)
    def _():
        scores = dot(keys_ref[...], query_ref[...], NT)
        s = lax.broadcasted_iota(jnp.int32, scores.shape, 0)
        t = lax.broadcasted_iota(jnp.int32, scores.shape, 1)
        score_ref[...] = jnp.where(s <= t, scores, 0.0)

    gate = gate_ref[...].astype(f32)
    silu_ref[...] = (gate / (1.0 + jnp.exp(-gate))).T

    s = lax.broadcasted_iota(jnp.int32, (half, half), 0)
    t = lax.broadcasted_iota(jnp.int32, (half, half), 1)
    differ = s ^ t
    low = score_ref[:half, :half]
    cross = score_ref[:half, half:]
    high = score_ref[half:, half:]
    for h in range(heads):
        w = w_ref[:, h, :].astype(f32)

        def mix(level, lo):
            return jnp.broadcast_to(w[level : level + 1, lo : lo + half], (half, half))

        def diagonal(lo, scores):
            m = mix(0, lo)
            for level in range(1, LOCAL_LEVELS - 1):
                m = jnp.where(differ >= (1 << (level - 1)), mix(level, lo), m)
            return (m * scores).astype(bf16)

        vt = vt_ref[h * size : (h + 1) * size, :]
        skip = skip_ref[first + h]
        near = dot(vt[:, :half], diagonal(0, low), NN)
        right = jnp.concatenate(
            [(mix(LOCAL_LEVELS - 1, half) * cross).astype(bf16), diagonal(half, high)], axis=0
        )
        far = dot(vt, right, NN)
        rows = slice(h * size, (h + 1) * size)
        acc_ref[rows, :half] = near + skip * vt[:, :half].astype(f32)
        acc_ref[rows, half:] = far + skip * vt[:, half:].astype(f32)


def local_part(vt, gate, keys, query, weights, skip, head_size):
    cols, tok = vt.shape
    n = keys.shape[1]
    heads = 8
    rows = heads * head_size
    steps = cols // rows
    return pl.pallas_call(
        functools.partial(local_kernel, heads, tok // 2),
        grid=(steps,),
        in_specs=[
            pl.BlockSpec(memory_space=pltpu.SMEM),
            pl.BlockSpec((rows, tok), lambda i: (i, 0)),
            pl.BlockSpec((tok, rows), lambda i: (0, i)),
            pl.BlockSpec((tok, n), lambda i: (0, 0)),
            pl.BlockSpec((tok, n), lambda i: (0, 0)),
            pl.BlockSpec((16, heads, tok), lambda i: (0, i, 0)),
        ],
        out_specs=[
            pl.BlockSpec((rows, tok), lambda i: (i, 0)),
            pl.BlockSpec((rows, tok), lambda i: (i, 0)),
        ],
        out_shape=[jax.ShapeDtypeStruct((cols, tok), f32)] * 2,
        scratch_shapes=[pltpu.VMEM((tok, tok), f32)],
        compiler_params=params(24),
        cost_estimate=cost(8 * tok * tok * cols, 12 * tok * cols),
        name="local_part",
    )(skip, vt, gate, keys, query, weights)


def pack_kernel(heads, slot, upper_ref, query_ref, w_ref, out_ref):
    n, tok = query_ref.shape[1], out_ref.shape[1]
    out_ref[:n] = query_ref[...].T
    count = upper_ref.shape[0]
    for e in range(w_ref.shape[1] // heads):
        rows = [
            w_ref[LOCAL_LEVELS + level, e * heads : (e + 1) * heads, :].astype(f32) * upper_ref[level]
            for level in range(count)
        ]
        rows.append(jnp.zeros((slot - count * heads, tok), f32))
        first = n + e * slot
        out_ref[first : first + slot] = jnp.concatenate(rows, axis=0).astype(bf16)


def packed(uppers, query, weights, heads, slot):
    tok, n = query.shape
    total = n + weights.shape[1] // heads * slot
    vmem = pl.BlockSpec(memory_space=pltpu.VMEM)
    return pl.pallas_call(
        functools.partial(pack_kernel, heads, slot),
        in_specs=[pl.BlockSpec(memory_space=pltpu.SMEM), vmem, vmem],
        out_specs=vmem,
        out_shape=jax.ShapeDtypeStruct((total, tok), bf16),
        compiler_params=pltpu.CompilerParams(vmem_limit_bytes=24 * 2**20),
        cost_estimate=cost(total * tok, 4 * total * tok),
        name="pack",
    )(uppers, query, weights)


def message_of(ref, j, share, n, slot):
    first = pl.multiple_of(n + share * slot, slot)
    return ref[j, :n, :], ref[j, pl.ds(first, slot), :].astype(f32)


def read_level(state, message, level, heads):
    query, weights = message
    rows, tok = state.shape[0], query.shape[1]
    part = dot(state, query, NN).reshape(heads, rows // heads, tok)
    return (part * weights[level * heads : (level + 1) * heads][:, None, :]).reshape(rows, tok)


def sibling_sum(ref, index, bit):
    count = 1 << bit
    first = ((index >> bit) ^ 1) << bit
    if count == 1:
        return ref[first]
    total = ref[first].astype(f32)
    for k in range(1, count):
        total = total + ref[first + k].astype(f32)
    return total.astype(bf16)


def low_kernel(heads, slot, where_ref, raw_ref, line_ref, message_ref, out_ref):
    n = raw_ref.shape[2]
    group = raw_ref.shape[0]
    local = {}
    for bit in range(3):
        for block in range(0, group, 2 << bit):
            local[bit, block] = sibling_sum(raw_ref, block + (1 << bit), bit)
    shared = [sibling_sum(line_ref, where_ref[0], bit) for bit in range(2)]
    for j in range(group):
        message = message_of(message_ref, j, where_ref[2], n, slot)
        total = read_level(shared[0], message, 3, heads)
        total = total + read_level(shared[1], message, 4, heads)
        for bit in range(3):
            if j >> bit & 1:
                block = j >> (bit + 1) << (bit + 1)
                total = total + read_level(local[bit, block], message, bit, heads)
        out_ref[j] = total


def high_kernel(heads, slot, where_ref, part_ref, plane_ref, message_ref, out_ref):
    n = plane_ref.shape[2]
    shared = [sibling_sum(plane_ref, where_ref[1], bit) for bit in range(2)]
    for j in range(part_ref.shape[0]):
        message = message_of(message_ref, j, where_ref[2], n, slot)
        total = part_ref[j] + read_level(shared[0], message, 5, heads)
        total = total + read_level(shared[1], message, 6, heads)
        out_ref[j] = total.astype(bf16)


def far_call(kernel, name, heads, slot, where, first, states, message, dtype):
    group, _, tok = message.shape
    rows = states.shape[1]
    vmem = pl.BlockSpec(memory_space=pltpu.VMEM)
    return pl.pallas_call(
        functools.partial(kernel, heads, slot),
        in_specs=[pl.BlockSpec(memory_space=pltpu.SMEM), vmem, vmem, vmem],
        out_specs=vmem,
        out_shape=jax.ShapeDtypeStruct((group, rows, tok), dtype),
        compiler_params=pltpu.CompilerParams(vmem_limit_bytes=24 * 2**20),
        cost_estimate=cost(8 * group * rows * tok * 128, 8 * group * rows * tok),
        name=name,
    )(where, first, states, message)


def project(where_ref, pieces, normed_ref, out_ref):
    mine = where_ref[1]
    half = normed_ref.shape[1]
    width = pieces[0].shape[1]
    for k in range(len(pieces) // 2):
        block = dot(pieces[2 * k][0], normed_ref[mine], NN)
        block = block + dot(pieces[2 * k + 1][0], normed_ref[1 - mine], NN)
        at = pl.multiple_of((where_ref[0] ^ k) * width, width)
        out_ref[:, pl.ds(at, width)] = block.T.astype(out_ref.dtype)


def finish_kernel(where_ref, *refs):
    pieces = refs[:8]
    acc_ref, silu_ref, far_ref, gain_ref, out_ref, normed_ref = refs[8:]

    @pl.when(pl.program_id(0) == 0)
    def _():
        rows = acc_ref.shape[0]
        gated = (acc_ref[...] + far_ref[...].astype(f32)) * silu_ref[...]
        squares = jnp.sum(gated * gated, axis=0, keepdims=True)
        scale = lax.rsqrt(squares / rows + epsilon)
        normed = (gated * scale * gain_ref[...]).astype(bf16)
        normed_ref[0] = normed[: rows // 2]
        normed_ref[1] = normed[rows // 2 :]

    project(where_ref, pieces, normed_ref, out_ref)


def keep_kernel(where_ref, *refs):
    project(where_ref, refs[:8], refs[8], refs[9])


def piece_specs(pieces, offset):
    _, cols, depth = pieces[0].shape
    return [
        pl.BlockSpec((1, cols, depth), lambda i, where: ((where[offset] + i) ^ where[4], 0, 0))
        for _ in pieces
    ]


def finish(where, pieces, acc, silu, far, gain):
    rows, tok = acc.shape
    z_size, cols, depth = pieces[0].shape
    steps = z_size // 2
    wide = cols * len(pieces) // 2

    def whole(array):
        return pl.BlockSpec(array.shape, lambda i, where: (0,) * array.ndim)

    others = [acc, silu, far, gain]
    return pl.pallas_call(
        finish_kernel,
        grid_spec=pltpu.PrefetchScalarGridSpec(
            num_scalar_prefetch=1,
            grid=(steps,),
            in_specs=piece_specs(pieces, 2) + [whole(a) for a in others],
            out_specs=[
                pl.BlockSpec((tok, wide), lambda i, where: (0, i)),
                pl.BlockSpec((2, rows // 2, tok), lambda i, where: (0, 0, 0)),
            ],
        ),
        out_shape=[
            jax.ShapeDtypeStruct((tok, wide * steps), bf16),
            jax.ShapeDtypeStruct((2, rows // 2, tok), bf16),
        ],
        compiler_params=params(40),
        cost_estimate=cost(2 * tok * rows * wide * steps, 16 * 2**20),
        name="finish",
    )(where, *pieces, *others)


def keep(where, pieces, normed):
    _, rows, tok = normed.shape
    z_size, cols, depth = pieces[0].shape
    steps = z_size // 2
    wide = cols * len(pieces) // 2
    return pl.pallas_call(
        keep_kernel,
        grid_spec=pltpu.PrefetchScalarGridSpec(
            num_scalar_prefetch=1,
            grid=(steps,),
            in_specs=piece_specs(pieces, 3)
            + [pl.BlockSpec((2, rows, tok), lambda i, where: (0, 0, 0))],
            out_specs=pl.BlockSpec((tok, wide), lambda i, where: (0, i)),
        ),
        out_shape=jax.ShapeDtypeStruct((tok, wide * steps), f32),
        compiler_params=params(40),
        cost_estimate=cost(2 * tok * 2 * rows * wide * steps, 8 * 2**20),
        name="keep",
    )(where, *pieces, normed)


def shared_along(value, axis):
    spread = jnp.broadcast_to(value[None], (lax.axis_size(axis), *value.shape))
    return lax.all_to_all(spread, axis, 0, 0, tiled=True)


def weight_line(out_weight):
    rows, cols = out_weight.shape
    mine = lax.axis_index("rep")
    half = lax.dynamic_slice_in_dim(out_weight, mine * (rows // 2), rows // 2, 0).T
    return shared_along(half, "y").reshape(-1, rows // 2)


def weight_pieces(line):
    own = jnp.stack([line] + [swapped(line, "zl", d) for d in range(1, lax.axis_size("zl"))])
    pieces = []
    for k in range(lax.axis_size("x")):
        piece = own if k == 0 else swapped(own, "x", k)
        pieces += [piece, swapped(piece, "rep", 1)]
    return pieces


def on_device(
    seq_values, seq_gate, seq_keys, seq_queries, level_weights, skip_gain, norm_gain, out_weight
):
    tok, width = seq_values.shape
    n = seq_keys.shape[1]
    head_count = skip_gain.shape[0]
    head_size = width // head_count
    group = lax.axis_size("y")
    heads = head_count // group
    rows = width // group
    slot = 32
    axes = [("y", b) for b in range(3)] + [("x", b) for b in range(2)] + [("zl", b) for b in range(2)]
    uppers = jnp.stack([(lax.axis_index(a) >> b) & 1 for a, b in axes]).astype(f32)
    x, y, z, head = (lax.axis_index(a) for a in ("x", "y", "zl", "head"))
    z_half = lax.axis_size("zl") // 2
    place = jnp.stack([x, z, y]).astype(jnp.int32)
    where = jnp.stack(
        [x, lax.axis_index("rep"), (1 - head) * z_half, head * z_half, z]
    ).astype(jnp.int32)

    weight = weight_line(out_weight)
    message = packed(uppers, seq_queries, level_weights, heads, slot)
    message = lax.all_gather(message, "y", axis=0)
    vt, sent = own_state(seq_values, seq_keys)
    sent, weight = lax.optimization_barrier((sent, weight))
    raw = lax.all_to_all(sent.reshape(group, rows, n), "y", 0, 0, tiled=True)
    pieces = weight_pieces(weight)
    acc, silu = local_part(vt, seq_gate, seq_keys, seq_queries, level_weights, skip_gain, head_size)
    raw, acc, silu = lax.optimization_barrier((raw, acc, silu))

    def summed(blocks):
        return jnp.sum(blocks.astype(f32), axis=0).astype(bf16)

    line = shared_along(summed(raw), "x")
    plane = shared_along(summed(line), "zl")
    part = far_call(low_kernel, "low_levels", heads, slot, place, raw, line, message, f32)
    far = far_call(high_kernel, "high_levels", heads, slot, place, part, plane, message, bf16)
    far = lax.all_to_all(far, "y", 0, 0, tiled=True).reshape(width, tok)

    to_send, normed = finish(where, pieces, acc, silu, far, norm_gain[:, None])
    got = swapped(to_send, "head", 1)
    kept = keep(where, pieces, normed)
    return (kept + got.astype(f32)).astype(bf16)


def solution(mesh):
    grid = Mesh(mesh.devices.reshape(4, 4, 8, 2, 2), ("zl", "x", "y", "head", "rep"))
    ctx = ("zl", "x", "y")
    tokens = ("rep", *ctx)
    placed = (
        P(tokens, "head"),
        P(tokens, "head"),
        P(tokens, None),
        P(tokens, None),
        P(None, "head", tokens),
        P("head"),
        P("head"),
        P("head", ctx),
    )
    return jax.shard_map(
        on_device, mesh=grid, in_specs=placed, out_specs=P(tokens, "head"), check_vma=False
    )
```

```python
import functools

import jax
import jax.numpy as jnp
from jax import lax
from jax.experimental import pallas as pl
from jax.experimental.pallas import tpu as pltpu
from jax.sharding import Mesh, PartitionSpec as P

epsilon = 1e-05
LOCAL_LEVELS = 9
VMEM_MIB = 56
NN = (((1,), (0,)), ((), ()))
NT = (((1,), (1,)), ((), ()))
f32 = jnp.float32
bf16 = jnp.bfloat16


def params(mib, steps=1):
    return pltpu.CompilerParams(
        vmem_limit_bytes=mib * 2**20, dimension_semantics=("arbitrary",) * steps
    )


def cost(flops, moved):
    return pl.CostEstimate(flops=flops, bytes_accessed=moved, transcendentals=0)


def swapped(value, axis, mask):
    return lax.ppermute(value, axis, [(i, i ^ mask) for i in range(lax.axis_size(axis))])


def dot(a, b, dims):
    return lax.dot_general(a, b, dims, preferred_element_type=f32)


def send_kernel(heads, slot, upper_ref, values_ref, keys_ref, query_ref, w_ref, vt_ref, sent_ref):
    vt = values_ref[...].T
    vt_ref[...] = vt
    state = dot(vt, keys_ref[...], NN).astype(bf16)
    tok, n = query_ref.shape
    count = upper_ref.shape[0]
    shares = sent_ref.shape[0]
    rows = state.shape[0] // shares
    for e in range(shares):
        w = [
            w_ref[LOCAL_LEVELS + level, e * heads : (e + 1) * heads, :].astype(f32) * upper_ref[level]
            for level in range(count)
        ]
        w.append(jnp.zeros((slot - count * heads, tok), f32))
        w = jnp.concatenate(w, axis=0).astype(bf16)
        sent_ref[e, :rows] = state[e * rows : (e + 1) * rows]
        sent_ref[e, rows : rows + tok] = query_ref[...]
        for k in range(tok // n):
            first = rows + tok + k * slot
            sent_ref[e, first : first + slot] = w[:, k * n : (k + 1) * n]


def to_group(uppers, values, keys, query, weights, group, slot):
    tok, width = values.shape
    n = keys.shape[1]
    steps = 4
    cols = width // steps
    heads = weights.shape[1] // group
    rows = width // group + tok + tok // n * slot
    return pl.pallas_call(
        functools.partial(send_kernel, heads, slot),
        grid=(steps,),
        in_specs=[
            pl.BlockSpec(memory_space=pltpu.SMEM),
            pl.BlockSpec((tok, cols), lambda i: (0, i)),
            pl.BlockSpec((tok, n), lambda i: (0, 0)),
            pl.BlockSpec((tok, n), lambda i: (0, 0)),
            pl.BlockSpec((16, group // steps * heads, tok), lambda i: (0, i, 0)),
        ],
        out_specs=[
            pl.BlockSpec((cols, tok), lambda i: (i, 0)),
            pl.BlockSpec((group // steps, rows, n), lambda i: (i, 0, 0)),
        ],
        out_shape=[
            jax.ShapeDtypeStruct((width, tok), bf16),
            jax.ShapeDtypeStruct((group, rows, n), bf16),
        ],
        compiler_params=params(VMEM_MIB),
        cost_estimate=cost(2 * tok * width * n, 4 * tok * width),
        name="to_group",
    )(uppers, values, keys, query, weights)


def local_kernel(heads, half, skip_ref, vt_ref, gate_ref, keys_ref, query_ref, w_ref, acc_ref, silu_ref, score_ref):
    size = vt_ref.shape[0] // heads
    first = pl.program_id(0) * heads

    @pl.when(pl.program_id(0) == 0)
    def _():
        scores = dot(keys_ref[...], query_ref[...], NT)
        s = lax.broadcasted_iota(jnp.int32, scores.shape, 0)
        t = lax.broadcasted_iota(jnp.int32, scores.shape, 1)
        score_ref[...] = jnp.where(s <= t, scores, 0.0)

    gate = gate_ref[...].astype(f32)
    silu_ref[...] = (gate / (1.0 + jnp.exp(-gate))).T

    s = lax.broadcasted_iota(jnp.int32, (half, half), 0)
    t = lax.broadcasted_iota(jnp.int32, (half, half), 1)
    differ = s ^ t
    low = score_ref[:half, :half]
    cross = score_ref[:half, half:]
    high = score_ref[half:, half:]
    for h in range(heads):
        w = w_ref[:, h, :].astype(f32)

        def mix(level, lo):
            return jnp.broadcast_to(w[level : level + 1, lo : lo + half], (half, half))

        def diagonal(lo, scores):
            m = mix(0, lo)
            for level in range(1, LOCAL_LEVELS - 1):
                m = jnp.where(differ >= (1 << (level - 1)), mix(level, lo), m)
            return (m * scores).astype(bf16)

        vt = vt_ref[h * size : (h + 1) * size, :]
        skip = skip_ref[first + h]
        near = dot(vt[:, :half], diagonal(0, low), NN)
        right = jnp.concatenate(
            [(mix(LOCAL_LEVELS - 1, half) * cross).astype(bf16), diagonal(half, high)], axis=0
        )
        far = dot(vt, right, NN)
        rows = slice(h * size, (h + 1) * size)
        acc_ref[rows, :half] = near + skip * vt[:, :half].astype(f32)
        acc_ref[rows, half:] = far + skip * vt[:, half:].astype(f32)


def local_part(vt, gate, keys, query, weights, skip, head_size):
    cols, tok = vt.shape
    n = keys.shape[1]
    heads = 8
    rows = heads * head_size
    steps = cols // rows
    return pl.pallas_call(
        functools.partial(local_kernel, heads, tok // 2),
        grid=(steps,),
        in_specs=[
            pl.BlockSpec(memory_space=pltpu.SMEM),
            pl.BlockSpec((rows, tok), lambda i: (i, 0)),
            pl.BlockSpec((tok, rows), lambda i: (0, i)),
            pl.BlockSpec((tok, n), lambda i: (0, 0)),
            pl.BlockSpec((tok, n), lambda i: (0, 0)),
            pl.BlockSpec((16, heads, tok), lambda i: (0, i, 0)),
        ],
        out_specs=[
            pl.BlockSpec((rows, tok), lambda i: (i, 0)),
            pl.BlockSpec((rows, tok), lambda i: (i, 0)),
        ],
        out_shape=[jax.ShapeDtypeStruct((cols, tok), f32)] * 2,
        scratch_shapes=[pltpu.VMEM((tok, tok), f32)],
        compiler_params=params(VMEM_MIB),
        cost_estimate=cost(8 * tok * tok * cols, 12 * tok * cols),
        name="local_part",
    )(skip, vt, gate, keys, query, weights)


def read_level(state, query, weights, level, heads):
    rows, tok = state.shape[0], query.shape[0]
    part = dot(state, query, NT).reshape(heads, rows // heads, tok)
    return (part * weights[level * heads : (level + 1) * heads][:, None, :]).reshape(rows, tok)


def sibling_sum(ref, index, bit, rows):
    count = 1 << bit
    first = ((index >> bit) ^ 1) << bit
    if count == 1:
        return ref[first, :rows]
    total = ref[first, :rows].astype(f32)
    for k in range(1, count):
        total = total + ref[first + k, :rows].astype(f32)
    return total.astype(bf16)


def far_kernel(heads, slot, where_ref, got_ref, line_ref, plane_ref, out_ref):
    group, rows, tok = out_ref.shape
    n = got_ref.shape[2]
    local = {}
    for bit in range(3):
        for block in range(0, group, 2 << bit):
            local[bit, block] = sibling_sum(got_ref, block + (1 << bit), bit, rows)
    shared = [sibling_sum(line_ref, where_ref[0], bit, rows) for bit in range(2)]
    shared += [sibling_sum(plane_ref, where_ref[1], bit, rows) for bit in range(2)]
    for j in range(group):
        query = got_ref[j, rows : rows + tok]
        weights = jnp.concatenate(
            [
                got_ref[j, rows + tok + k * slot : rows + tok + (k + 1) * slot]
                for k in range(tok // n)
            ],
            axis=1,
        ).astype(f32)
        total = read_level(shared[0], query, weights, 3, heads)
        for level in range(1, 4):
            total = total + read_level(shared[level], query, weights, 3 + level, heads)
        for bit in range(3):
            if j >> bit & 1:
                block = j >> (bit + 1) << (bit + 1)
                total = total + read_level(local[bit, block], query, weights, bit, heads)
        out_ref[j] = total.astype(bf16)


def far_levels(where, got, line, plane, heads, slot, tok):
    group = got.shape[0]
    rows = line.shape[1]
    vmem = pl.BlockSpec(memory_space=pltpu.VMEM)
    return pl.pallas_call(
        functools.partial(far_kernel, heads, slot),
        in_specs=[pl.BlockSpec(memory_space=pltpu.SMEM), vmem, vmem, vmem],
        out_specs=vmem,
        out_shape=jax.ShapeDtypeStruct((group, rows, tok), bf16),
        compiler_params=pltpu.CompilerParams(vmem_limit_bytes=VMEM_MIB * 2**20),
        cost_estimate=cost(12 * group * rows * tok * 128, 8 * group * rows * tok),
        name="far_levels",
    )(where, got, line, plane)


def project(where_ref, pieces, normed_ref, out_ref):
    mine = where_ref[1]
    half = normed_ref.shape[1]
    width = pieces[0].shape[1]
    for k in range(len(pieces) // 2):
        block = dot(pieces[2 * k][0], normed_ref[mine], NN)
        block = block + dot(pieces[2 * k + 1][0], normed_ref[1 - mine], NN)
        at = pl.multiple_of((where_ref[0] ^ k) * width, width)
        out_ref[:, pl.ds(at, width)] = block.T.astype(out_ref.dtype)


def finish_kernel(where_ref, *refs):
    pieces = refs[:8]
    acc_ref, silu_ref, far_ref, gain_ref, out_ref, normed_ref = refs[8:]

    @pl.when(pl.program_id(0) == 0)
    def _():
        rows = acc_ref.shape[0]
        gated = (acc_ref[...] + far_ref[...].astype(f32)) * silu_ref[...]
        squares = jnp.sum(gated * gated, axis=0, keepdims=True)
        scale = lax.rsqrt(squares / rows + epsilon)
        normed = (gated * scale * gain_ref[...]).astype(bf16)
        normed_ref[0] = normed[: rows // 2]
        normed_ref[1] = normed[rows // 2 :]

    project(where_ref, pieces, normed_ref, out_ref)


def keep_kernel(where_ref, *refs):
    project(where_ref, refs[:8], refs[8], refs[9])


def piece_specs(pieces, offset):
    _, cols, depth = pieces[0].shape
    return [
        pl.BlockSpec((1, cols, depth), lambda i, where: ((where[offset] + i) ^ where[4], 0, 0))
        for _ in pieces
    ]


def finish(where, pieces, acc, silu, far, gain):
    rows, tok = acc.shape
    z_size, cols, depth = pieces[0].shape
    steps = z_size // 2
    wide = cols * len(pieces) // 2

    def whole(array):
        return pl.BlockSpec(array.shape, lambda i, where: (0,) * array.ndim)

    others = [acc, silu, far, gain]
    return pl.pallas_call(
        finish_kernel,
        grid_spec=pltpu.PrefetchScalarGridSpec(
            num_scalar_prefetch=1,
            grid=(steps,),
            in_specs=piece_specs(pieces, 2) + [whole(a) for a in others],
            out_specs=[
                pl.BlockSpec((tok, wide), lambda i, where: (0, i)),
                pl.BlockSpec((2, rows // 2, tok), lambda i, where: (0, 0, 0)),
            ],
        ),
        out_shape=[
            jax.ShapeDtypeStruct((tok, wide * steps), bf16),
            jax.ShapeDtypeStruct((2, rows // 2, tok), bf16),
        ],
        compiler_params=params(max(VMEM_MIB, 40)),
        cost_estimate=cost(2 * tok * rows * wide * steps, 16 * 2**20),
        name="finish",
    )(where, *pieces, *others)


def keep(where, pieces, normed):
    _, rows, tok = normed.shape
    z_size, cols, depth = pieces[0].shape
    steps = z_size // 2
    wide = cols * len(pieces) // 2
    return pl.pallas_call(
        keep_kernel,
        grid_spec=pltpu.PrefetchScalarGridSpec(
            num_scalar_prefetch=1,
            grid=(steps,),
            in_specs=piece_specs(pieces, 3)
            + [pl.BlockSpec((2, rows, tok), lambda i, where: (0, 0, 0))],
            out_specs=pl.BlockSpec((tok, wide), lambda i, where: (0, i)),
        ),
        out_shape=jax.ShapeDtypeStruct((tok, wide * steps), f32),
        compiler_params=params(max(VMEM_MIB, 40)),
        cost_estimate=cost(2 * tok * 2 * rows * wide * steps, 8 * 2**20),
        name="keep",
    )(where, *pieces, normed)


def shared_along(value, axis):
    spread = jnp.broadcast_to(value[None], (lax.axis_size(axis), *value.shape))
    return lax.all_to_all(spread, axis, 0, 0, tiled=True)


def weight_line(out_weight):
    rows, cols = out_weight.shape
    mine = lax.axis_index("rep")
    half = lax.dynamic_slice_in_dim(out_weight, mine * (rows // 2), rows // 2, 0).T
    return shared_along(half, "y").reshape(-1, rows // 2)


def weight_plane(line):
    return jnp.stack([line] + [swapped(line, "zl", d) for d in range(1, lax.axis_size("zl"))])


def weight_pieces(own):
    pieces = []
    for k in range(lax.axis_size("x")):
        piece = own if k == 0 else swapped(own, "x", k)
        pieces += [piece, swapped(piece, "rep", 1)]
    return pieces


def on_device(
    seq_values, seq_gate, seq_keys, seq_queries, level_weights, skip_gain, norm_gain, out_weight
):
    tok, width = seq_values.shape
    n = seq_keys.shape[1]
    head_count = skip_gain.shape[0]
    head_size = width // head_count
    group = lax.axis_size("y")
    heads = head_count // group
    rows = width // group
    slot = 32
    axes = [("y", b) for b in range(3)] + [("x", b) for b in range(2)] + [("zl", b) for b in range(2)]
    uppers = jnp.stack([(lax.axis_index(a) >> b) & 1 for a, b in axes]).astype(f32)
    x, y, z, head = (lax.axis_index(a) for a in ("x", "y", "zl", "head"))
    z_half = lax.axis_size("zl") // 2
    place = jnp.stack([x, z]).astype(jnp.int32)
    where = jnp.stack(
        [x, lax.axis_index("rep"), (1 - head) * z_half, head * z_half, z]
    ).astype(jnp.int32)

    weight = weight_line(out_weight)
    vt, sent = to_group(uppers, seq_values, seq_keys, seq_queries, level_weights, group, slot)
    sent, weight = lax.optimization_barrier((sent, weight))
    raw = lax.all_to_all(sent, "y", 0, 0, tiled=True)
    weight = weight_plane(weight)
    acc, silu = local_part(vt, seq_gate, seq_keys, seq_queries, level_weights, skip_gain, head_size)
    raw, acc, silu, weight = lax.optimization_barrier((raw, acc, silu, weight))
    pieces = weight_pieces(weight)

    def summed(blocks):
        return jnp.sum(blocks.astype(f32), axis=0).astype(bf16)

    line = shared_along(summed(raw[:, :rows]), "x")
    plane = shared_along(summed(line), "zl")
    far = far_levels(place, raw, line, plane, heads, slot, tok)
    far = lax.all_to_all(far, "y", 0, 0, tiled=True).reshape(width, tok)

    to_send, normed = finish(where, pieces, acc, silu, far, norm_gain[:, None])
    got = swapped(to_send, "head", 1)
    kept = keep(where, pieces, normed)
    return (kept + got.astype(f32)).astype(bf16)


def solution(mesh):
    grid = Mesh(mesh.devices.reshape(4, 4, 8, 2, 2), ("zl", "x", "y", "head", "rep"))
    ctx = ("zl", "x", "y")
    tokens = ("rep", *ctx)
    placed = (
        P(tokens, "head"),
        P(tokens, "head"),
        P(tokens, None),
        P(tokens, None),
        P(None, "head", tokens),
        P("head"),
        P("head"),
        P("head", ctx),
    )
    return jax.shard_map(
        on_device, mesh=grid, in_specs=placed, out_specs=P(tokens, "head"), check_vma=False
    )
```

```python
import functools

import jax
import jax.numpy as jnp
from jax import lax
from jax.experimental import pallas as pl
from jax.experimental.pallas import tpu as pltpu
from jax.sharding import Mesh, PartitionSpec as P

epsilon = 1e-05
LOCAL_LEVELS = 9
VMEM_MIB = 56
NN = (((1,), (0,)), ((), ()))
NT = (((1,), (1,)), ((), ()))
f32 = jnp.float32
bf16 = jnp.bfloat16


def params(mib, steps=1):
    return pltpu.CompilerParams(
        vmem_limit_bytes=mib * 2**20, dimension_semantics=("arbitrary",) * steps
    )


def cost(flops, moved):
    return pl.CostEstimate(flops=flops, bytes_accessed=moved, transcendentals=0)


def swapped(value, axis, mask):
    return lax.ppermute(value, axis, [(i, i ^ mask) for i in range(lax.axis_size(axis))])


def dot(a, b, dims):
    return lax.dot_general(a, b, dims, preferred_element_type=f32)


def send_kernel(heads, slot, upper_ref, values_ref, keys_ref, query_ref, w_ref, vt_ref, sent_ref):
    vt = values_ref[...].T
    vt_ref[...] = vt
    state = dot(vt, keys_ref[...], NN).astype(bf16)
    tok, n = query_ref.shape
    count = upper_ref.shape[0]
    shares = sent_ref.shape[0]
    rows = state.shape[0] // shares
    for e in range(shares):
        w = [
            w_ref[LOCAL_LEVELS + level, e * heads : (e + 1) * heads, :].astype(f32) * upper_ref[level]
            for level in range(count)
        ]
        w.append(jnp.zeros((slot - count * heads, tok), f32))
        w = jnp.concatenate(w, axis=0).astype(bf16)
        sent_ref[e, :rows] = state[e * rows : (e + 1) * rows]
        sent_ref[e, rows : rows + tok] = query_ref[...]
        for k in range(tok // n):
            first = rows + tok + k * slot
            sent_ref[e, first : first + slot] = w[:, k * n : (k + 1) * n]


def to_group(uppers, values, keys, query, weights, group, slot):
    tok, width = values.shape
    n = keys.shape[1]
    steps = 4
    cols = width // steps
    heads = weights.shape[1] // group
    rows = width // group + tok + tok // n * slot
    return pl.pallas_call(
        functools.partial(send_kernel, heads, slot),
        grid=(steps,),
        in_specs=[
            pl.BlockSpec(memory_space=pltpu.SMEM),
            pl.BlockSpec((tok, cols), lambda i: (0, i)),
            pl.BlockSpec((tok, n), lambda i: (0, 0)),
            pl.BlockSpec((tok, n), lambda i: (0, 0)),
            pl.BlockSpec((16, group // steps * heads, tok), lambda i: (0, i, 0)),
        ],
        out_specs=[
            pl.BlockSpec((cols, tok), lambda i: (i, 0)),
            pl.BlockSpec((group // steps, rows, n), lambda i: (i, 0, 0)),
        ],
        out_shape=[
            jax.ShapeDtypeStruct((width, tok), bf16),
            jax.ShapeDtypeStruct((group, rows, n), bf16),
        ],
        compiler_params=params(VMEM_MIB),
        cost_estimate=cost(2 * tok * width * n, 4 * tok * width),
        name="to_group",
    )(uppers, values, keys, query, weights)


def local_kernel(heads, half, skip_ref, vt_ref, gate_ref, keys_ref, query_ref, w_ref, acc_ref, silu_ref, score_ref):
    size = vt_ref.shape[0] // heads
    first = pl.program_id(0) * heads

    @pl.when(pl.program_id(0) == 0)
    def _():
        scores = dot(keys_ref[...], query_ref[...], NT)
        s = lax.broadcasted_iota(jnp.int32, scores.shape, 0)
        t = lax.broadcasted_iota(jnp.int32, scores.shape, 1)
        score_ref[...] = jnp.where(s <= t, scores, 0.0)

    gate = gate_ref[...].astype(f32)
    silu_ref[...] = (gate / (1.0 + jnp.exp(-gate))).T

    s = lax.broadcasted_iota(jnp.int32, (half, half), 0)
    t = lax.broadcasted_iota(jnp.int32, (half, half), 1)
    differ = s ^ t
    low = score_ref[:half, :half]
    cross = score_ref[:half, half:]
    high = score_ref[half:, half:]
    for h in range(heads):
        w = w_ref[:, h, :].astype(f32)

        def mix(level, lo):
            return jnp.broadcast_to(w[level : level + 1, lo : lo + half], (half, half))

        def diagonal(lo, scores):
            m = mix(0, lo)
            for level in range(1, LOCAL_LEVELS - 1):
                m = jnp.where(differ >= (1 << (level - 1)), mix(level, lo), m)
            return (m * scores).astype(bf16)

        vt = vt_ref[h * size : (h + 1) * size, :]
        skip = skip_ref[first + h]
        near = dot(vt[:, :half], diagonal(0, low), NN)
        right = jnp.concatenate(
            [(mix(LOCAL_LEVELS - 1, half) * cross).astype(bf16), diagonal(half, high)], axis=0
        )
        far = dot(vt, right, NN)
        rows = slice(h * size, (h + 1) * size)
        acc_ref[rows, :half] = near + skip * vt[:, :half].astype(f32)
        acc_ref[rows, half:] = far + skip * vt[:, half:].astype(f32)


def local_part(vt, gate, keys, query, weights, skip, head_size):
    cols, tok = vt.shape
    n = keys.shape[1]
    heads = 8
    rows = heads * head_size
    steps = cols // rows
    return pl.pallas_call(
        functools.partial(local_kernel, heads, tok // 2),
        grid=(steps,),
        in_specs=[
            pl.BlockSpec(memory_space=pltpu.SMEM),
            pl.BlockSpec((rows, tok), lambda i: (i, 0)),
            pl.BlockSpec((tok, rows), lambda i: (0, i)),
            pl.BlockSpec((tok, n), lambda i: (0, 0)),
            pl.BlockSpec((tok, n), lambda i: (0, 0)),
            pl.BlockSpec((16, heads, tok), lambda i: (0, i, 0)),
        ],
        out_specs=[
            pl.BlockSpec((rows, tok), lambda i: (i, 0)),
            pl.BlockSpec((rows, tok), lambda i: (i, 0)),
        ],
        out_shape=[jax.ShapeDtypeStruct((cols, tok), f32)] * 2,
        scratch_shapes=[pltpu.VMEM((tok, tok), f32)],
        compiler_params=params(VMEM_MIB),
        cost_estimate=cost(8 * tok * tok * cols, 12 * tok * cols),
        name="local_part",
    )(skip, vt, gate, keys, query, weights)


def read_level(state, query, weights, level, heads):
    rows, tok = state.shape[0], query.shape[0]
    part = dot(state, query, NT).reshape(heads, rows // heads, tok)
    return (part * weights[level * heads : (level + 1) * heads][:, None, :]).reshape(rows, tok)


def sibling_sum(ref, index, bit, rows):
    count = 1 << bit
    first = ((index >> bit) ^ 1) << bit
    if count == 1:
        return ref[first, :rows]
    total = ref[first, :rows].astype(f32)
    for k in range(1, count):
        total = total + ref[first + k, :rows].astype(f32)
    return total.astype(bf16)


def far_kernel(heads, slot, where_ref, got_ref, line_ref, plane_ref, out_ref):
    group, rows, tok = out_ref.shape
    n = got_ref.shape[2]
    local = {}
    for bit in range(3):
        for block in range(0, group, 2 << bit):
            local[bit, block] = sibling_sum(got_ref, block + (1 << bit), bit, rows)
    shared = [sibling_sum(line_ref, where_ref[0], bit, rows) for bit in range(2)]
    shared += [sibling_sum(plane_ref, where_ref[1], bit, rows) for bit in range(2)]
    for j in range(group):
        query = got_ref[j, rows : rows + tok]
        weights = jnp.concatenate(
            [
                got_ref[j, rows + tok + k * slot : rows + tok + (k + 1) * slot]
                for k in range(tok // n)
            ],
            axis=1,
        ).astype(f32)
        total = read_level(shared[0], query, weights, 3, heads)
        for level in range(1, 4):
            total = total + read_level(shared[level], query, weights, 3 + level, heads)
        for bit in range(3):
            if j >> bit & 1:
                block = j >> (bit + 1) << (bit + 1)
                total = total + read_level(local[bit, block], query, weights, bit, heads)
        out_ref[j] = total.astype(bf16)


def far_levels(where, got, line, plane, heads, slot, tok):
    group = got.shape[0]
    rows = line.shape[1]
    vmem = pl.BlockSpec(memory_space=pltpu.VMEM)
    return pl.pallas_call(
        functools.partial(far_kernel, heads, slot),
        in_specs=[pl.BlockSpec(memory_space=pltpu.SMEM), vmem, vmem, vmem],
        out_specs=vmem,
        out_shape=jax.ShapeDtypeStruct((group, rows, tok), bf16),
        compiler_params=pltpu.CompilerParams(vmem_limit_bytes=VMEM_MIB * 2**20),
        cost_estimate=cost(12 * group * rows * tok * 128, 8 * group * rows * tok),
        name="far_levels",
    )(where, got, line, plane)


def project(where_ref, pieces, normed_ref, out_ref):
    mine = where_ref[1]
    half = normed_ref.shape[1]
    width = pieces[0].shape[1]
    for k in range(len(pieces) // 2):
        block = dot(pieces[2 * k][0], normed_ref[mine], NN)
        block = block + dot(pieces[2 * k + 1][0], normed_ref[1 - mine], NN)
        at = pl.multiple_of((where_ref[0] ^ k) * width, width)
        out_ref[:, pl.ds(at, width)] = block.T.astype(out_ref.dtype)


def finish_kernel(where_ref, *refs):
    pieces = refs[:8]
    acc_ref, silu_ref, far_ref, gain_ref, out_ref, normed_ref = refs[8:]

    @pl.when(pl.program_id(0) == 0)
    def _():
        rows = acc_ref.shape[0]
        gated = (acc_ref[...] + far_ref[...].astype(f32)) * silu_ref[...]
        squares = jnp.sum(gated * gated, axis=0, keepdims=True)
        scale = lax.rsqrt(squares / rows + epsilon)
        normed = (gated * scale * gain_ref[...]).astype(bf16)
        normed_ref[0] = normed[: rows // 2]
        normed_ref[1] = normed[rows // 2 :]

    project(where_ref, pieces, normed_ref, out_ref)


def keep_kernel(where_ref, *refs):
    project(where_ref, refs[:8], refs[8], refs[9])


def piece_specs(pieces, offset):
    _, cols, depth = pieces[0].shape
    return [
        pl.BlockSpec((1, cols, depth), lambda i, where: ((where[offset] + i) ^ where[4], 0, 0))
        for _ in pieces
    ]


def finish(where, pieces, acc, silu, far, gain):
    rows, tok = acc.shape
    z_size, cols, depth = pieces[0].shape
    steps = z_size // 2
    wide = cols * len(pieces) // 2

    def whole(array):
        return pl.BlockSpec(array.shape, lambda i, where: (0,) * array.ndim)

    others = [acc, silu, far, gain]
    return pl.pallas_call(
        finish_kernel,
        grid_spec=pltpu.PrefetchScalarGridSpec(
            num_scalar_prefetch=1,
            grid=(steps,),
            in_specs=piece_specs(pieces, 2) + [whole(a) for a in others],
            out_specs=[
                pl.BlockSpec((tok, wide), lambda i, where: (0, i)),
                pl.BlockSpec((2, rows // 2, tok), lambda i, where: (0, 0, 0)),
            ],
        ),
        out_shape=[
            jax.ShapeDtypeStruct((tok, wide * steps), bf16),
            jax.ShapeDtypeStruct((2, rows // 2, tok), bf16),
        ],
        compiler_params=params(max(VMEM_MIB, 40)),
        cost_estimate=cost(2 * tok * rows * wide * steps, 16 * 2**20),
        name="finish",
    )(where, *pieces, *others)


def keep(where, pieces, normed):
    _, rows, tok = normed.shape
    z_size, cols, depth = pieces[0].shape
    steps = z_size // 2
    wide = cols * len(pieces) // 2
    return pl.pallas_call(
        keep_kernel,
        grid_spec=pltpu.PrefetchScalarGridSpec(
            num_scalar_prefetch=1,
            grid=(steps,),
            in_specs=piece_specs(pieces, 3)
            + [pl.BlockSpec((2, rows, tok), lambda i, where: (0, 0, 0))],
            out_specs=pl.BlockSpec((tok, wide), lambda i, where: (0, i)),
        ),
        out_shape=jax.ShapeDtypeStruct((tok, wide * steps), f32),
        compiler_params=params(max(VMEM_MIB, 40)),
        cost_estimate=cost(2 * tok * 2 * rows * wide * steps, 8 * 2**20),
        name="keep",
    )(where, *pieces, normed)


def shared_along(value, axis):
    spread = jnp.broadcast_to(value[None], (lax.axis_size(axis), *value.shape))
    return lax.all_to_all(spread, axis, 0, 0, tiled=True)


def weight_line(out_weight):
    rows, cols = out_weight.shape
    mine = lax.axis_index("rep")
    half = lax.dynamic_slice_in_dim(out_weight, mine * (rows // 2), rows // 2, 0).T
    return shared_along(half, "y").reshape(-1, rows // 2)


def weight_plane(line):
    return jnp.stack([line] + [swapped(line, "zl", d) for d in range(1, lax.axis_size("zl"))])


def weight_pieces(halves):
    pieces = []
    for piece in halves:
        pieces += [piece, swapped(piece, "rep", 1)]
    return pieces


def on_device(
    seq_values, seq_gate, seq_keys, seq_queries, level_weights, skip_gain, norm_gain, out_weight
):
    tok, width = seq_values.shape
    n = seq_keys.shape[1]
    head_count = skip_gain.shape[0]
    head_size = width // head_count
    group = lax.axis_size("y")
    heads = head_count // group
    rows = width // group
    slot = 32
    axes = [("y", b) for b in range(3)] + [("x", b) for b in range(2)] + [("zl", b) for b in range(2)]
    uppers = jnp.stack([(lax.axis_index(a) >> b) & 1 for a, b in axes]).astype(f32)
    x, y, z, head = (lax.axis_index(a) for a in ("x", "y", "zl", "head"))
    z_half = lax.axis_size("zl") // 2
    place = jnp.stack([x, z]).astype(jnp.int32)
    where = jnp.stack(
        [x, lax.axis_index("rep"), (1 - head) * z_half, head * z_half, z]
    ).astype(jnp.int32)

    weight = weight_line(out_weight)
    vt, sent = to_group(uppers, seq_values, seq_keys, seq_queries, level_weights, group, slot)
    sent, weight = lax.optimization_barrier((sent, weight))
    raw = lax.all_to_all(sent, "y", 0, 0, tiled=True)
    weight = weight_plane(weight)
    acc, silu = local_part(vt, seq_gate, seq_keys, seq_queries, level_weights, skip_gain, head_size)
    raw, acc, silu, own = lax.optimization_barrier((raw, acc, silu, weight))
    near, middle, last = [swapped(weight, "x", k) for k in range(1, lax.axis_size("x"))]

    def summed(blocks):
        return jnp.sum(blocks.astype(f32), axis=0).astype(bf16)

    line = shared_along(summed(raw[:, :rows]), "x")
    plane = shared_along(summed(line), "zl")
    plane, own, near, last = lax.optimization_barrier((plane, own, near, last))
    pieces = weight_pieces([own, near, middle, last])
    far = far_levels(place, raw, line, plane, heads, slot, tok)
    far = lax.all_to_all(far, "y", 0, 0, tiled=True).reshape(width, tok)

    to_send, normed = finish(where, pieces, acc, silu, far, norm_gain[:, None])
    got = swapped(to_send, "head", 1)
    kept = keep(where, pieces, normed)
    return (kept + got.astype(f32)).astype(bf16)


def solution(mesh):
    grid = Mesh(mesh.devices.reshape(4, 4, 8, 2, 2), ("zl", "x", "y", "head", "rep"))
    ctx = ("zl", "x", "y")
    tokens = ("rep", *ctx)
    placed = (
        P(tokens, "head"),
        P(tokens, "head"),
        P(tokens, None),
        P(tokens, None),
        P(None, "head", tokens),
        P("head"),
        P("head"),
        P("head", ctx),
    )
    return jax.shard_map(
        on_device, mesh=grid, in_specs=placed, out_specs=P(tokens, "head"), check_vma=False
    )
```

```python
import functools

import jax
import jax.numpy as jnp
from jax import lax
from jax.experimental import pallas as pl
from jax.experimental.pallas import tpu as pltpu
from jax.sharding import Mesh, PartitionSpec as P

epsilon = 1e-05
LOCAL_LEVELS = 9
VMEM_MIB = 56
NN = (((1,), (0,)), ((), ()))
NT = (((1,), (1,)), ((), ()))
f32 = jnp.float32
bf16 = jnp.bfloat16


def params(mib, steps=1):
    return pltpu.CompilerParams(
        vmem_limit_bytes=mib * 2**20, dimension_semantics=("arbitrary",) * steps
    )


def cost(flops, moved):
    return pl.CostEstimate(flops=flops, bytes_accessed=moved, transcendentals=0)


def swapped(value, axis, mask):
    return lax.ppermute(value, axis, [(i, i ^ mask) for i in range(lax.axis_size(axis))])


def dot(a, b, dims):
    return lax.dot_general(a, b, dims, preferred_element_type=f32)


def send_kernel(heads, slot, upper_ref, values_ref, keys_ref, query_ref, w_ref, vt_ref, sent_ref):
    vt = values_ref[...].T
    vt_ref[...] = vt
    state = dot(vt, keys_ref[...], NN).astype(bf16)
    tok, n = query_ref.shape
    count = upper_ref.shape[0]
    shares = sent_ref.shape[0]
    rows = state.shape[0] // shares
    for e in range(shares):
        w = [
            w_ref[LOCAL_LEVELS + level, e * heads : (e + 1) * heads, :].astype(f32) * upper_ref[level]
            for level in range(count)
        ]
        w.append(jnp.zeros((slot - count * heads, tok), f32))
        w = jnp.concatenate(w, axis=0).astype(bf16)
        sent_ref[e, :rows] = state[e * rows : (e + 1) * rows]
        sent_ref[e, rows : rows + tok] = query_ref[...]
        for k in range(tok // n):
            first = rows + tok + k * slot
            sent_ref[e, first : first + slot] = w[:, k * n : (k + 1) * n]


def to_group(uppers, values, keys, query, weights, group, slot):
    tok, width = values.shape
    n = keys.shape[1]
    steps = 4
    cols = width // steps
    heads = weights.shape[1] // group
    rows = width // group + tok + tok // n * slot
    return pl.pallas_call(
        functools.partial(send_kernel, heads, slot),
        grid=(steps,),
        in_specs=[
            pl.BlockSpec(memory_space=pltpu.SMEM),
            pl.BlockSpec((tok, cols), lambda i: (0, i)),
            pl.BlockSpec((tok, n), lambda i: (0, 0)),
            pl.BlockSpec((tok, n), lambda i: (0, 0)),
            pl.BlockSpec((16, group // steps * heads, tok), lambda i: (0, i, 0)),
        ],
        out_specs=[
            pl.BlockSpec((cols, tok), lambda i: (i, 0)),
            pl.BlockSpec((group // steps, rows, n), lambda i: (i, 0, 0)),
        ],
        out_shape=[
            jax.ShapeDtypeStruct((width, tok), bf16),
            jax.ShapeDtypeStruct((group, rows, n), bf16),
        ],
        compiler_params=params(VMEM_MIB),
        cost_estimate=cost(2 * tok * width * n, 4 * tok * width),
        name="to_group",
    )(uppers, values, keys, query, weights)


def local_kernel(heads, half, skip_ref, vt_ref, gate_ref, keys_ref, query_ref, w_ref, acc_ref, silu_ref, score_ref):
    size = vt_ref.shape[0] // heads
    first = pl.program_id(0) * heads

    @pl.when(pl.program_id(0) == 0)
    def _():
        scores = dot(keys_ref[...], query_ref[...], NT)
        s = lax.broadcasted_iota(jnp.int32, scores.shape, 0)
        t = lax.broadcasted_iota(jnp.int32, scores.shape, 1)
        score_ref[...] = jnp.where(s <= t, scores, 0.0)

    gate = gate_ref[...].astype(f32)
    silu_ref[...] = (gate / (1.0 + jnp.exp(-gate))).T

    s = lax.broadcasted_iota(jnp.int32, (half, half), 0)
    t = lax.broadcasted_iota(jnp.int32, (half, half), 1)
    differ = s ^ t
    low = score_ref[:half, :half]
    cross = score_ref[:half, half:]
    high = score_ref[half:, half:]
    for h in range(heads):
        w = w_ref[:, h, :].astype(f32)

        def mix(level, lo):
            return jnp.broadcast_to(w[level : level + 1, lo : lo + half], (half, half))

        def diagonal(lo, scores):
            m = mix(0, lo)
            for level in range(1, LOCAL_LEVELS - 1):
                m = jnp.where(differ >= (1 << (level - 1)), mix(level, lo), m)
            return (m * scores).astype(bf16)

        vt = vt_ref[h * size : (h + 1) * size, :]
        skip = skip_ref[first + h]
        near = dot(vt[:, :half], diagonal(0, low), NN)
        right = jnp.concatenate(
            [(mix(LOCAL_LEVELS - 1, half) * cross).astype(bf16), diagonal(half, high)], axis=0
        )
        far = dot(vt, right, NN)
        rows = slice(h * size, (h + 1) * size)
        acc_ref[rows, :half] = near + skip * vt[:, :half].astype(f32)
        acc_ref[rows, half:] = far + skip * vt[:, half:].astype(f32)


def local_part(vt, gate, keys, query, weights, skip, head_size):
    cols, tok = vt.shape
    n = keys.shape[1]
    heads = 8
    rows = heads * head_size
    steps = cols // rows
    return pl.pallas_call(
        functools.partial(local_kernel, heads, tok // 2),
        grid=(steps,),
        in_specs=[
            pl.BlockSpec(memory_space=pltpu.SMEM),
            pl.BlockSpec((rows, tok), lambda i: (i, 0)),
            pl.BlockSpec((tok, rows), lambda i: (0, i)),
            pl.BlockSpec((tok, n), lambda i: (0, 0)),
            pl.BlockSpec((tok, n), lambda i: (0, 0)),
            pl.BlockSpec((16, heads, tok), lambda i: (0, i, 0)),
        ],
        out_specs=[
            pl.BlockSpec((rows, tok), lambda i: (i, 0)),
            pl.BlockSpec((rows, tok), lambda i: (i, 0)),
        ],
        out_shape=[jax.ShapeDtypeStruct((cols, tok), f32)] * 2,
        scratch_shapes=[pltpu.VMEM((tok, tok), f32)],
        compiler_params=params(VMEM_MIB),
        cost_estimate=cost(8 * tok * tok * cols, 12 * tok * cols),
        name="local_part",
    )(skip, vt, gate, keys, query, weights)


def read_level(state, query, weights, level, heads):
    rows, tok = state.shape[0], query.shape[0]
    part = dot(state, query, NT).reshape(heads, rows // heads, tok)
    return (part * weights[level * heads : (level + 1) * heads][:, None, :]).reshape(rows, tok)


def sibling_sum(ref, index, bit, rows):
    count = 1 << bit
    first = ((index >> bit) ^ 1) << bit
    if count == 1:
        return ref[first, :rows]
    total = ref[first, :rows].astype(f32)
    for k in range(1, count):
        total = total + ref[first + k, :rows].astype(f32)
    return total.astype(bf16)


def far_kernel(heads, slot, where_ref, got_ref, line_ref, plane_ref, out_ref):
    group, rows, tok = out_ref.shape
    n = got_ref.shape[2]
    local = {}
    for bit in range(3):
        for block in range(0, group, 2 << bit):
            local[bit, block] = sibling_sum(got_ref, block + (1 << bit), bit, rows)
    shared = [sibling_sum(line_ref, where_ref[0], bit, rows) for bit in range(2)]
    shared += [sibling_sum(plane_ref, where_ref[1], bit, rows) for bit in range(2)]
    for j in range(group):
        query = got_ref[j, rows : rows + tok]
        weights = jnp.concatenate(
            [
                got_ref[j, rows + tok + k * slot : rows + tok + (k + 1) * slot]
                for k in range(tok // n)
            ],
            axis=1,
        ).astype(f32)
        total = read_level(shared[0], query, weights, 3, heads)
        for level in range(1, 4):
            total = total + read_level(shared[level], query, weights, 3 + level, heads)
        for bit in range(3):
            if j >> bit & 1:
                block = j >> (bit + 1) << (bit + 1)
                total = total + read_level(local[bit, block], query, weights, bit, heads)
        out_ref[j] = total.astype(bf16)


def far_levels(where, got, line, plane, heads, slot, tok):
    group = got.shape[0]
    rows = line.shape[1]
    vmem = pl.BlockSpec(memory_space=pltpu.VMEM)
    return pl.pallas_call(
        functools.partial(far_kernel, heads, slot),
        in_specs=[pl.BlockSpec(memory_space=pltpu.SMEM), vmem, vmem, vmem],
        out_specs=vmem,
        out_shape=jax.ShapeDtypeStruct((group, rows, tok), bf16),
        compiler_params=pltpu.CompilerParams(vmem_limit_bytes=VMEM_MIB * 2**20),
        cost_estimate=cost(12 * group * rows * tok * 128, 8 * group * rows * tok),
        name="far_levels",
    )(where, got, line, plane)


def project(where_ref, pieces, normed_ref, out_ref):
    mine = where_ref[1]
    half = normed_ref.shape[1]
    width = pieces[0].shape[1]
    for k in range(len(pieces) // 2):
        block = dot(pieces[2 * k][0], normed_ref[mine], NN)
        block = block + dot(pieces[2 * k + 1][0], normed_ref[1 - mine], NN)
        at = pl.multiple_of((where_ref[0] ^ k) * width, width)
        out_ref[:, pl.ds(at, width)] = block.T.astype(out_ref.dtype)


def finish_kernel(where_ref, *refs):
    pieces = refs[:8]
    acc_ref, silu_ref, far_ref, gain_ref, out_ref, normed_ref = refs[8:]

    @pl.when(pl.program_id(0) == 0)
    def _():
        rows = acc_ref.shape[0]
        gated = (acc_ref[...] + far_ref[...].astype(f32)) * silu_ref[...]
        squares = jnp.sum(gated * gated, axis=0, keepdims=True)
        scale = lax.rsqrt(squares / rows + epsilon)
        normed = (gated * scale * gain_ref[...]).astype(bf16)
        normed_ref[0] = normed[: rows // 2]
        normed_ref[1] = normed[rows // 2 :]

    project(where_ref, pieces, normed_ref, out_ref)


def keep_kernel(where_ref, *refs):
    project(where_ref, refs[:8], refs[8], refs[9])


def piece_specs(pieces, offset):
    _, cols, depth = pieces[0].shape
    return [
        pl.BlockSpec((1, cols, depth), lambda i, where: ((where[offset] + i) ^ where[4], 0, 0))
        for _ in pieces
    ]


def finish(where, pieces, acc, silu, far, gain):
    rows, tok = acc.shape
    z_size, cols, depth = pieces[0].shape
    steps = z_size // 2
    wide = cols * len(pieces) // 2

    def whole(array):
        return pl.BlockSpec(array.shape, lambda i, where: (0,) * array.ndim)

    others = [acc, silu, far, gain]
    return pl.pallas_call(
        finish_kernel,
        grid_spec=pltpu.PrefetchScalarGridSpec(
            num_scalar_prefetch=1,
            grid=(steps,),
            in_specs=piece_specs(pieces, 2) + [whole(a) for a in others],
            out_specs=[
                pl.BlockSpec((tok, wide), lambda i, where: (0, i)),
                pl.BlockSpec((2, rows // 2, tok), lambda i, where: (0, 0, 0)),
            ],
        ),
        out_shape=[
            jax.ShapeDtypeStruct((tok, wide * steps), bf16),
            jax.ShapeDtypeStruct((2, rows // 2, tok), bf16),
        ],
        compiler_params=params(40),
        cost_estimate=cost(2 * tok * rows * wide * steps, 16 * 2**20),
        name="finish",
    )(where, *pieces, *others)


def keep(where, pieces, normed):
    _, rows, tok = normed.shape
    z_size, cols, depth = pieces[0].shape
    steps = z_size // 2
    wide = cols * len(pieces) // 2
    return pl.pallas_call(
        keep_kernel,
        grid_spec=pltpu.PrefetchScalarGridSpec(
            num_scalar_prefetch=1,
            grid=(steps,),
            in_specs=piece_specs(pieces, 3)
            + [pl.BlockSpec((2, rows, tok), lambda i, where: (0, 0, 0))],
            out_specs=pl.BlockSpec((tok, wide), lambda i, where: (0, i)),
        ),
        out_shape=jax.ShapeDtypeStruct((tok, wide * steps), f32),
        compiler_params=params(40),
        cost_estimate=cost(2 * tok * 2 * rows * wide * steps, 8 * 2**20),
        name="keep",
    )(where, *pieces, normed)


def shared_along(value, axis):
    spread = jnp.broadcast_to(value[None], (lax.axis_size(axis), *value.shape))
    return lax.all_to_all(spread, axis, 0, 0, tiled=True)


def weight_line(out_weight):
    rows, cols = out_weight.shape
    mine = lax.axis_index("rep")
    half = lax.dynamic_slice_in_dim(out_weight, mine * (rows // 2), rows // 2, 0).T
    return shared_along(half, "y").reshape(-1, rows // 2)


def weight_pieces(halves):
    pieces = []
    for piece in halves:
        pieces += [piece, swapped(piece, "rep", 1)]
    return pieces


def on_device(
    seq_values, seq_gate, seq_keys, seq_queries, level_weights, skip_gain, norm_gain, out_weight
):
    tok, width = seq_values.shape
    n = seq_keys.shape[1]
    head_count = skip_gain.shape[0]
    head_size = width // head_count
    group = lax.axis_size("y")
    heads = head_count // group
    rows = width // group
    slot = 32
    axes = [("y", b) for b in range(3)] + [("x", b) for b in range(2)] + [("zl", b) for b in range(2)]
    uppers = jnp.stack([(lax.axis_index(a) >> b) & 1 for a, b in axes]).astype(f32)
    x, y, z, head = (lax.axis_index(a) for a in ("x", "y", "zl", "head"))
    z_half = lax.axis_size("zl") // 2
    place = jnp.stack([x, z]).astype(jnp.int32)
    where = jnp.stack(
        [x, lax.axis_index("rep"), (1 - head) * z_half, head * z_half, z]
    ).astype(jnp.int32)

    weight = weight_line(out_weight)
    vt, sent = to_group(uppers, seq_values, seq_keys, seq_queries, level_weights, group, slot)
    sent, weight = lax.optimization_barrier((sent, weight))
    raw = lax.all_to_all(sent, "y", 0, 0, tiled=True)
    planes = [swapped(weight, "zl", d) for d in range(1, lax.axis_size("zl"))]
    acc, silu = local_part(vt, seq_gate, seq_keys, seq_queries, level_weights, skip_gain, head_size)
    planes, acc, silu = lax.optimization_barrier((planes, acc, silu))
    own = jnp.stack([weight, *planes])
    near, middle, last = [swapped(own, "x", k) for k in range(1, lax.axis_size("x"))]
    raw, own = lax.optimization_barrier((raw, own))

    def summed(blocks):
        return jnp.sum(blocks.astype(f32), axis=0).astype(bf16)

    line = shared_along(summed(raw[:, :rows]), "x")
    plane = shared_along(summed(line), "zl")
    plane, own, near, last = lax.optimization_barrier((plane, own, near, last))
    pieces = weight_pieces([own, near, middle, last])
    far = far_levels(place, raw, line, plane, heads, slot, tok)
    far = lax.all_to_all(far, "y", 0, 0, tiled=True).reshape(width, tok)

    to_send, normed = finish(where, pieces, acc, silu, far, norm_gain[:, None])
    got = swapped(to_send, "head", 1)
    kept = keep(where, pieces, normed)
    return (kept + got.astype(f32)).astype(bf16)


def solution(mesh):
    grid = Mesh(mesh.devices.reshape(4, 4, 8, 2, 2), ("zl", "x", "y", "head", "rep"))
    ctx = ("zl", "x", "y")
    tokens = ("rep", *ctx)
    placed = (
        P(tokens, "head"),
        P(tokens, "head"),
        P(tokens, None),
        P(tokens, None),
        P(None, "head", tokens),
        P("head"),
        P("head"),
        P("head", ctx),
    )
    return jax.shard_map(
        on_device, mesh=grid, in_specs=placed, out_specs=P(tokens, "head"), check_vma=False
    )
```

```python
import functools

import jax
import jax.numpy as jnp
from jax import lax
from jax.experimental import pallas as pl
from jax.experimental.pallas import tpu as pltpu
from jax.sharding import Mesh, PartitionSpec as P

epsilon = 1e-05
LOCAL_LEVELS = 9
VMEM_MIB = 56
NN = (((1,), (0,)), ((), ()))
NT = (((1,), (1,)), ((), ()))
f32 = jnp.float32
bf16 = jnp.bfloat16


def params(mib, steps=1):
    return pltpu.CompilerParams(
        vmem_limit_bytes=mib * 2**20, dimension_semantics=("arbitrary",) * steps
    )


def cost(flops, moved):
    return pl.CostEstimate(flops=flops, bytes_accessed=moved, transcendentals=0)


def swapped(value, axis, mask):
    return lax.ppermute(value, axis, [(i, i ^ mask) for i in range(lax.axis_size(axis))])


def dot(a, b, dims):
    return lax.dot_general(a, b, dims, preferred_element_type=f32)


def send_kernel(heads, slot, upper_ref, values_ref, keys_ref, query_ref, w_ref, vt_ref, sent_ref):
    vt = values_ref[...].T
    vt_ref[...] = vt
    state = dot(vt, keys_ref[...], NN).astype(bf16)
    tok, n = query_ref.shape
    count = upper_ref.shape[0]
    shares = sent_ref.shape[0]
    rows = state.shape[0] // shares
    for e in range(shares):
        w = [
            w_ref[LOCAL_LEVELS + level, e * heads : (e + 1) * heads, :].astype(f32) * upper_ref[level]
            for level in range(count)
        ]
        w.append(jnp.zeros((slot - count * heads, tok), f32))
        w = jnp.concatenate(w, axis=0).astype(bf16)
        sent_ref[e, :rows] = state[e * rows : (e + 1) * rows]
        sent_ref[e, rows : rows + tok] = query_ref[...]
        for k in range(tok // n):
            first = rows + tok + k * slot
            sent_ref[e, first : first + slot] = w[:, k * n : (k + 1) * n]


def to_group(uppers, values, keys, query, weights, group, slot):
    tok, width = values.shape
    n = keys.shape[1]
    steps = 4
    cols = width // steps
    heads = weights.shape[1] // group
    rows = width // group + tok + tok // n * slot
    return pl.pallas_call(
        functools.partial(send_kernel, heads, slot),
        grid=(steps,),
        in_specs=[
            pl.BlockSpec(memory_space=pltpu.SMEM),
            pl.BlockSpec((tok, cols), lambda i: (0, i)),
            pl.BlockSpec((tok, n), lambda i: (0, 0)),
            pl.BlockSpec((tok, n), lambda i: (0, 0)),
            pl.BlockSpec((16, group // steps * heads, tok), lambda i: (0, i, 0)),
        ],
        out_specs=[
            pl.BlockSpec((cols, tok), lambda i: (i, 0)),
            pl.BlockSpec((group // steps, rows, n), lambda i: (i, 0, 0)),
        ],
        out_shape=[
            jax.ShapeDtypeStruct((width, tok), bf16),
            jax.ShapeDtypeStruct((group, rows, n), bf16),
        ],
        compiler_params=params(VMEM_MIB),
        cost_estimate=cost(2 * tok * width * n, 4 * tok * width),
        name="to_group",
    )(uppers, values, keys, query, weights)


def local_kernel(heads, half, skip_ref, vt_ref, gate_ref, keys_ref, query_ref, w_ref, acc_ref, silu_ref, score_ref):
    size = vt_ref.shape[0] // heads
    first = pl.program_id(0) * heads

    @pl.when(pl.program_id(0) == 0)
    def _():
        scores = dot(keys_ref[...], query_ref[...], NT)
        s = lax.broadcasted_iota(jnp.int32, scores.shape, 0)
        t = lax.broadcasted_iota(jnp.int32, scores.shape, 1)
        score_ref[...] = jnp.where(s <= t, scores, 0.0)

    gate = gate_ref[...].astype(f32)
    silu_ref[...] = (gate / (1.0 + jnp.exp(-gate))).T

    s = lax.broadcasted_iota(jnp.int32, (half, half), 0)
    t = lax.broadcasted_iota(jnp.int32, (half, half), 1)
    differ = s ^ t
    low = score_ref[:half, :half]
    cross = score_ref[:half, half:]
    high = score_ref[half:, half:]
    for h in range(heads):
        w = w_ref[:, h, :].astype(f32)

        def mix(level, lo):
            return jnp.broadcast_to(w[level : level + 1, lo : lo + half], (half, half))

        def diagonal(lo, scores):
            m = mix(0, lo)
            for level in range(1, LOCAL_LEVELS - 1):
                m = jnp.where(differ >= (1 << (level - 1)), mix(level, lo), m)
            return (m * scores).astype(bf16)

        vt = vt_ref[h * size : (h + 1) * size, :]
        skip = skip_ref[first + h]
        near = dot(vt[:, :half], diagonal(0, low), NN)
        right = jnp.concatenate(
            [(mix(LOCAL_LEVELS - 1, half) * cross).astype(bf16), diagonal(half, high)], axis=0
        )
        far = dot(vt, right, NN)
        rows = slice(h * size, (h + 1) * size)
        acc_ref[rows, :half] = near + skip * vt[:, :half].astype(f32)
        acc_ref[rows, half:] = far + skip * vt[:, half:].astype(f32)


def local_part(vt, gate, keys, query, weights, skip, head_size):
    cols, tok = vt.shape
    n = keys.shape[1]
    heads = 8
    rows = heads * head_size
    steps = cols // rows
    return pl.pallas_call(
        functools.partial(local_kernel, heads, tok // 2),
        grid=(steps,),
        in_specs=[
            pl.BlockSpec(memory_space=pltpu.SMEM),
            pl.BlockSpec((rows, tok), lambda i: (i, 0)),
            pl.BlockSpec((tok, rows), lambda i: (0, i)),
            pl.BlockSpec((tok, n), lambda i: (0, 0)),
            pl.BlockSpec((tok, n), lambda i: (0, 0)),
            pl.BlockSpec((16, heads, tok), lambda i: (0, i, 0)),
        ],
        out_specs=[
            pl.BlockSpec((rows, tok), lambda i: (i, 0)),
            pl.BlockSpec((rows, tok), lambda i: (i, 0)),
        ],
        out_shape=[jax.ShapeDtypeStruct((cols, tok), f32)] * 2,
        scratch_shapes=[pltpu.VMEM((tok, tok), f32)],
        compiler_params=params(VMEM_MIB),
        cost_estimate=cost(8 * tok * tok * cols, 12 * tok * cols),
        name="local_part",
    )(skip, vt, gate, keys, query, weights)


def read_level(state, query, weights, level, heads):
    rows, tok = state.shape[0], query.shape[0]
    part = dot(state, query, NT).reshape(heads, rows // heads, tok)
    return (part * weights[level * heads : (level + 1) * heads][:, None, :]).reshape(rows, tok)


def total_of(parts):
    total = parts[0].astype(f32)
    for part in parts[1:]:
        total = total + part.astype(f32)
    return total.astype(bf16)


def siblings(index, bit):
    first = ((index >> bit) ^ 1) << bit
    return [first + k for k in range(1 << bit)]


def group_kernel(got_ref, out_ref):
    total = total_of([got_ref[j] for j in range(got_ref.shape[0])])
    for k in range(out_ref.shape[0]):
        out_ref[k] = total


def group_sum(got, rows, copies):
    group, _, n = got.shape
    return pl.pallas_call(
        group_kernel,
        grid=(1,),
        in_specs=[pl.BlockSpec((group, rows, n), lambda i: (0, 0, 0))],
        out_specs=pl.BlockSpec((copies, rows, n), lambda i: (0, 0, 0)),
        out_shape=jax.ShapeDtypeStruct((copies, rows, n), bf16),
        compiler_params=params(8),
        cost_estimate=cost(group * rows * n, 2 * (group + copies) * rows * n),
        name="group_sum",
    )(got)


def column_kernel(where_ref, line_ref, out_ref):
    z = where_ref[1]
    sums = [line_ref[z]]
    sums += [total_of([line_ref[i] for i in siblings(z, bit)]) for bit in range(2)]
    for k in range(out_ref.shape[0]):
        for i, value in enumerate(sums):
            out_ref[k, i] = value


def column_sums(where, line, copies):
    _, rows, n = line.shape
    vmem = pl.BlockSpec(memory_space=pltpu.VMEM)
    return pl.pallas_call(
        column_kernel,
        in_specs=[pl.BlockSpec(memory_space=pltpu.SMEM), vmem],
        out_specs=vmem,
        out_shape=jax.ShapeDtypeStruct((copies, 3, rows, n), bf16),
        compiler_params=pltpu.CompilerParams(vmem_limit_bytes=8 * 2**20),
        cost_estimate=cost(4 * rows * n, 2 * (4 + 3 * copies) * rows * n),
        name="column_sums",
    )(where, line)


def far_kernel(heads, slot, where_ref, got_ref, plane_ref, out_ref):
    group, rows, tok = out_ref.shape
    n = got_ref.shape[2]
    x = where_ref[0]
    local = {}
    for bit in range(3):
        for block in range(0, group, 2 << bit):
            parts = [got_ref[i, :rows] for i in siblings(block + (1 << bit), bit)]
            local[bit, block] = total_of(parts)
    shared = [total_of([plane_ref[i, 0] for i in siblings(x, bit)]) for bit in range(2)]
    for kind in (1, 2):
        shared.append(total_of([plane_ref[i, kind] for i in range(plane_ref.shape[0])]))
    for j in range(group):
        query = got_ref[j, rows : rows + tok]
        weights = jnp.concatenate(
            [
                got_ref[j, rows + tok + k * slot : rows + tok + (k + 1) * slot]
                for k in range(tok // n)
            ],
            axis=1,
        ).astype(f32)
        total = read_level(shared[0], query, weights, 3, heads)
        for level in range(1, 4):
            total = total + read_level(shared[level], query, weights, 3 + level, heads)
        for bit in range(3):
            if j >> bit & 1:
                block = j >> (bit + 1) << (bit + 1)
                total = total + read_level(local[bit, block], query, weights, bit, heads)
        out_ref[j] = total.astype(bf16)


def far_levels(where, got, plane, heads, slot, tok):
    group = got.shape[0]
    rows = plane.shape[2]
    vmem = pl.BlockSpec(memory_space=pltpu.VMEM)
    return pl.pallas_call(
        functools.partial(far_kernel, heads, slot),
        in_specs=[pl.BlockSpec(memory_space=pltpu.SMEM), vmem, vmem],
        out_specs=vmem,
        out_shape=jax.ShapeDtypeStruct((group, rows, tok), bf16),
        compiler_params=pltpu.CompilerParams(vmem_limit_bytes=VMEM_MIB * 2**20),
        cost_estimate=cost(12 * group * rows * tok * 128, 8 * group * rows * tok),
        name="far_levels",
    )(where, got, plane)


def project(where_ref, pieces, normed_ref, out_ref):
    mine = where_ref[1]
    half = normed_ref.shape[1]
    width = pieces[0].shape[1]
    for k in range(len(pieces) // 2):
        block = dot(pieces[2 * k][0], normed_ref[mine], NN)
        block = block + dot(pieces[2 * k + 1][0], normed_ref[1 - mine], NN)
        at = pl.multiple_of((where_ref[0] ^ k) * width, width)
        out_ref[:, pl.ds(at, width)] = block.T.astype(out_ref.dtype)


def finish_kernel(where_ref, *refs):
    pieces = refs[:8]
    acc_ref, silu_ref, far_ref, gain_ref, out_ref, normed_ref = refs[8:]

    @pl.when(pl.program_id(0) == 0)
    def _():
        rows = acc_ref.shape[0]
        gated = (acc_ref[...] + far_ref[...].astype(f32)) * silu_ref[...]
        squares = jnp.sum(gated * gated, axis=0, keepdims=True)
        scale = lax.rsqrt(squares / rows + epsilon)
        normed = (gated * scale * gain_ref[...]).astype(bf16)
        normed_ref[0] = normed[: rows // 2]
        normed_ref[1] = normed[rows // 2 :]

    project(where_ref, pieces, normed_ref, out_ref)


def keep_kernel(where_ref, *refs):
    project(where_ref, refs[:8], refs[8], refs[9])


def piece_specs(pieces, offset):
    _, cols, depth = pieces[0].shape
    return [
        pl.BlockSpec((1, cols, depth), lambda i, where: ((where[offset] + i) ^ where[4], 0, 0))
        for _ in pieces
    ]


def finish(where, pieces, acc, silu, far, gain):
    rows, tok = acc.shape
    z_size, cols, depth = pieces[0].shape
    steps = z_size // 2
    wide = cols * len(pieces) // 2

    def whole(array):
        return pl.BlockSpec(array.shape, lambda i, where: (0,) * array.ndim)

    others = [acc, silu, far, gain]
    return pl.pallas_call(
        finish_kernel,
        grid_spec=pltpu.PrefetchScalarGridSpec(
            num_scalar_prefetch=1,
            grid=(steps,),
            in_specs=piece_specs(pieces, 2) + [whole(a) for a in others],
            out_specs=[
                pl.BlockSpec((tok, wide), lambda i, where: (0, i)),
                pl.BlockSpec((2, rows // 2, tok), lambda i, where: (0, 0, 0)),
            ],
        ),
        out_shape=[
            jax.ShapeDtypeStruct((tok, wide * steps), bf16),
            jax.ShapeDtypeStruct((2, rows // 2, tok), bf16),
        ],
        compiler_params=params(40),
        cost_estimate=cost(2 * tok * rows * wide * steps, 16 * 2**20),
        name="finish",
    )(where, *pieces, *others)


def keep(where, pieces, normed):
    _, rows, tok = normed.shape
    z_size, cols, depth = pieces[0].shape
    steps = z_size // 2
    wide = cols * len(pieces) // 2
    return pl.pallas_call(
        keep_kernel,
        grid_spec=pltpu.PrefetchScalarGridSpec(
            num_scalar_prefetch=1,
            grid=(steps,),
            in_specs=piece_specs(pieces, 3)
            + [pl.BlockSpec((2, rows, tok), lambda i, where: (0, 0, 0))],
            out_specs=pl.BlockSpec((tok, wide), lambda i, where: (0, i)),
        ),
        out_shape=jax.ShapeDtypeStruct((tok, wide * steps), f32),
        compiler_params=params(40),
        cost_estimate=cost(2 * tok * 2 * rows * wide * steps, 8 * 2**20),
        name="keep",
    )(where, *pieces, normed)


def shared_along(value, axis):
    spread = jnp.broadcast_to(value[None], (lax.axis_size(axis), *value.shape))
    return lax.all_to_all(spread, axis, 0, 0, tiled=True)


def weight_line(out_weight):
    rows, cols = out_weight.shape
    mine = lax.axis_index("rep")
    half = lax.dynamic_slice_in_dim(out_weight, mine * (rows // 2), rows // 2, 0).T
    return shared_along(half, "y").reshape(-1, rows // 2)


def weight_pieces(halves):
    pieces = []
    for piece in halves:
        pieces += [piece, swapped(piece, "rep", 1)]
    return pieces


def on_device(
    seq_values, seq_gate, seq_keys, seq_queries, level_weights, skip_gain, norm_gain, out_weight
):
    tok, width = seq_values.shape
    n = seq_keys.shape[1]
    head_count = skip_gain.shape[0]
    head_size = width // head_count
    group = lax.axis_size("y")
    heads = head_count // group
    rows = width // group
    slot = 32
    axes = [("y", b) for b in range(3)] + [("x", b) for b in range(2)] + [("zl", b) for b in range(2)]
    uppers = jnp.stack([(lax.axis_index(a) >> b) & 1 for a, b in axes]).astype(f32)
    x, y, z, head = (lax.axis_index(a) for a in ("x", "y", "zl", "head"))
    z_half = lax.axis_size("zl") // 2
    place = jnp.stack([x, z]).astype(jnp.int32)
    where = jnp.stack(
        [x, lax.axis_index("rep"), (1 - head) * z_half, head * z_half, z]
    ).astype(jnp.int32)

    weight = weight_line(out_weight)
    vt, sent = to_group(uppers, seq_values, seq_keys, seq_queries, level_weights, group, slot)
    sent, weight = lax.optimization_barrier((sent, weight))
    raw = lax.all_to_all(sent, "y", 0, 0, tiled=True)
    planes = [swapped(weight, "zl", d) for d in range(1, lax.axis_size("zl"))]
    acc, silu = local_part(vt, seq_gate, seq_keys, seq_queries, level_weights, skip_gain, head_size)
    planes, acc, silu = lax.optimization_barrier((planes, acc, silu))
    own = jnp.stack([weight, *planes])
    near, middle, last = [swapped(own, "x", k) for k in range(1, lax.axis_size("x"))]
    raw, own = lax.optimization_barrier((raw, own))

    line = group_sum(raw, rows, lax.axis_size("zl"))
    line = lax.all_to_all(line, "zl", 0, 0, tiled=True)
    plane = column_sums(place, line, lax.axis_size("x"))
    plane = lax.all_to_all(plane, "x", 0, 0, tiled=True)
    plane, own, near, last = lax.optimization_barrier((plane, own, near, last))
    pieces = weight_pieces([own, near, middle, last])
    far = far_levels(place, raw, plane, heads, slot, tok)
    far = lax.all_to_all(far, "y", 0, 0, tiled=True).reshape(width, tok)

    to_send, normed = finish(where, pieces, acc, silu, far, norm_gain[:, None])
    got = swapped(to_send, "head", 1)
    kept = keep(where, pieces, normed)
    return (kept + got.astype(f32)).astype(bf16)


def solution(mesh):
    grid = Mesh(mesh.devices.reshape(4, 4, 8, 2, 2), ("zl", "x", "y", "head", "rep"))
    ctx = ("zl", "x", "y")
    tokens = ("rep", *ctx)
    placed = (
        P(tokens, "head"),
        P(tokens, "head"),
        P(tokens, None),
        P(tokens, None),
        P(None, "head", tokens),
        P("head"),
        P("head"),
        P("head", ctx),
    )
    return jax.shard_map(
        on_device, mesh=grid, in_specs=placed, out_specs=P(tokens, "head"), check_vma=False
    )
```

```python
import functools

import jax
import jax.numpy as jnp
from jax import lax
from jax.experimental import pallas as pl
from jax.experimental.pallas import tpu as pltpu
from jax.sharding import Mesh, PartitionSpec as P

epsilon = 1e-05
LOCAL_LEVELS = 9
VMEM_MIB = 56
NN = (((1,), (0,)), ((), ()))
NT = (((1,), (1,)), ((), ()))
f32 = jnp.float32
bf16 = jnp.bfloat16


def params(mib, steps=1):
    return pltpu.CompilerParams(
        vmem_limit_bytes=mib * 2**20, dimension_semantics=("arbitrary",) * steps
    )


def cost(flops, moved):
    return pl.CostEstimate(flops=flops, bytes_accessed=moved, transcendentals=0)


def swapped(value, axis, mask):
    return lax.ppermute(value, axis, [(i, i ^ mask) for i in range(lax.axis_size(axis))])


def dot(a, b, dims):
    return lax.dot_general(a, b, dims, preferred_element_type=f32)


def send_kernel(heads, slot, upper_ref, values_ref, keys_ref, query_ref, w_ref, vt_ref, sent_ref):
    vt = values_ref[...].T
    vt_ref[...] = vt
    state = dot(vt, keys_ref[...], NN).astype(bf16)
    tok, n = query_ref.shape
    count = upper_ref.shape[0]
    shares = sent_ref.shape[0]
    rows = state.shape[0] // shares
    for e in range(shares):
        w = [
            w_ref[LOCAL_LEVELS + level, e * heads : (e + 1) * heads, :].astype(f32) * upper_ref[level]
            for level in range(count)
        ]
        w.append(jnp.zeros((slot - count * heads, tok), f32))
        w = jnp.concatenate(w, axis=0).astype(bf16)
        sent_ref[e, :rows] = state[e * rows : (e + 1) * rows]
        sent_ref[e, rows : rows + tok] = query_ref[...]
        for k in range(tok // n):
            first = rows + tok + k * slot
            sent_ref[e, first : first + slot] = w[:, k * n : (k + 1) * n]


def to_group(uppers, values, keys, query, weights, group, slot):
    tok, width = values.shape
    n = keys.shape[1]
    steps = 4
    cols = width // steps
    heads = weights.shape[1] // group
    rows = width // group + tok + tok // n * slot
    return pl.pallas_call(
        functools.partial(send_kernel, heads, slot),
        grid=(steps,),
        in_specs=[
            pl.BlockSpec(memory_space=pltpu.SMEM),
            pl.BlockSpec((tok, cols), lambda i: (0, i)),
            pl.BlockSpec((tok, n), lambda i: (0, 0)),
            pl.BlockSpec((tok, n), lambda i: (0, 0)),
            pl.BlockSpec((16, group // steps * heads, tok), lambda i: (0, i, 0)),
        ],
        out_specs=[
            pl.BlockSpec((cols, tok), lambda i: (i, 0)),
            pl.BlockSpec((group // steps, rows, n), lambda i: (i, 0, 0)),
        ],
        out_shape=[
            jax.ShapeDtypeStruct((width, tok), bf16),
            jax.ShapeDtypeStruct((group, rows, n), bf16),
        ],
        compiler_params=params(VMEM_MIB),
        cost_estimate=cost(2 * tok * width * n, 4 * tok * width),
        name="to_group",
    )(uppers, values, keys, query, weights)


def local_kernel(heads, half, skip_ref, vt_ref, gate_ref, keys_ref, query_ref, w_ref, acc_ref, silu_ref, score_ref):
    size = vt_ref.shape[0] // heads
    first = pl.program_id(0) * heads

    @pl.when(pl.program_id(0) == 0)
    def _():
        scores = dot(keys_ref[...], query_ref[...], NT)
        s = lax.broadcasted_iota(jnp.int32, scores.shape, 0)
        t = lax.broadcasted_iota(jnp.int32, scores.shape, 1)
        score_ref[...] = jnp.where(s <= t, scores, 0.0)

    gate = gate_ref[...].astype(f32)
    silu_ref[...] = (gate / (1.0 + jnp.exp(-gate))).T

    s = lax.broadcasted_iota(jnp.int32, (half, half), 0)
    t = lax.broadcasted_iota(jnp.int32, (half, half), 1)
    differ = s ^ t
    low = score_ref[:half, :half]
    cross = score_ref[:half, half:]
    high = score_ref[half:, half:]
    for h in range(heads):
        w = w_ref[:, h, :].astype(f32)

        def mix(level, lo):
            return jnp.broadcast_to(w[level : level + 1, lo : lo + half], (half, half))

        def diagonal(lo, scores):
            m = mix(0, lo)
            for level in range(1, LOCAL_LEVELS - 1):
                m = jnp.where(differ >= (1 << (level - 1)), mix(level, lo), m)
            return (m * scores).astype(bf16)

        vt = vt_ref[h * size : (h + 1) * size, :]
        skip = skip_ref[first + h]
        near = dot(vt[:, :half], diagonal(0, low), NN)
        right = jnp.concatenate(
            [(mix(LOCAL_LEVELS - 1, half) * cross).astype(bf16), diagonal(half, high)], axis=0
        )
        far = dot(vt, right, NN)
        rows = slice(h * size, (h + 1) * size)
        acc_ref[rows, :half] = near + skip * vt[:, :half].astype(f32)
        acc_ref[rows, half:] = far + skip * vt[:, half:].astype(f32)


def local_part(vt, gate, keys, query, weights, skip, head_size):
    cols, tok = vt.shape
    n = keys.shape[1]
    heads = 8
    rows = heads * head_size
    steps = cols // rows
    return pl.pallas_call(
        functools.partial(local_kernel, heads, tok // 2),
        grid=(steps,),
        in_specs=[
            pl.BlockSpec(memory_space=pltpu.SMEM),
            pl.BlockSpec((rows, tok), lambda i: (i, 0)),
            pl.BlockSpec((tok, rows), lambda i: (0, i)),
            pl.BlockSpec((tok, n), lambda i: (0, 0)),
            pl.BlockSpec((tok, n), lambda i: (0, 0)),
            pl.BlockSpec((16, heads, tok), lambda i: (0, i, 0)),
        ],
        out_specs=[
            pl.BlockSpec((rows, tok), lambda i: (i, 0)),
            pl.BlockSpec((rows, tok), lambda i: (i, 0)),
        ],
        out_shape=[jax.ShapeDtypeStruct((cols, tok), f32)] * 2,
        scratch_shapes=[pltpu.VMEM((tok, tok), f32)],
        compiler_params=params(VMEM_MIB),
        cost_estimate=cost(8 * tok * tok * cols, 12 * tok * cols),
        name="local_part",
    )(skip, vt, gate, keys, query, weights)


def read_level(state, query, weights, level, heads):
    rows, tok = state.shape[0], query.shape[0]
    part = dot(state, query, NT).reshape(heads, rows // heads, tok)
    return (part * weights[level * heads : (level + 1) * heads][:, None, :]).reshape(rows, tok)


def total_of(parts):
    total = parts[0].astype(f32)
    for part in parts[1:]:
        total = total + part.astype(f32)
    return total.astype(bf16)


def siblings(index, bit):
    first = ((index >> bit) ^ 1) << bit
    return [first + k for k in range(1 << bit)]


def group_kernel(got_ref, out_ref):
    total = total_of([got_ref[j] for j in range(got_ref.shape[0])])
    for k in range(out_ref.shape[0]):
        out_ref[k] = total


def group_sum(got, rows, copies):
    group, _, n = got.shape
    return pl.pallas_call(
        group_kernel,
        grid=(1,),
        in_specs=[pl.BlockSpec((group, rows, n), lambda i: (0, 0, 0))],
        out_specs=pl.BlockSpec((copies, rows, n), lambda i: (0, 0, 0)),
        out_shape=jax.ShapeDtypeStruct((copies, rows, n), bf16),
        compiler_params=params(8),
        cost_estimate=cost(group * rows * n, 2 * (group + copies) * rows * n),
        name="group_sum",
    )(got)


def column_kernel(where_ref, line_ref, out_ref):
    z = where_ref[1]
    sums = [line_ref[z]]
    sums += [total_of([line_ref[i] for i in siblings(z, bit)]) for bit in range(2)]
    for k in range(out_ref.shape[0]):
        for i, value in enumerate(sums):
            out_ref[k, i] = value


def column_sums(where, line, copies):
    _, rows, n = line.shape
    vmem = pl.BlockSpec(memory_space=pltpu.VMEM)
    return pl.pallas_call(
        column_kernel,
        in_specs=[pl.BlockSpec(memory_space=pltpu.SMEM), vmem],
        out_specs=vmem,
        out_shape=jax.ShapeDtypeStruct((copies, 3, rows, n), bf16),
        compiler_params=pltpu.CompilerParams(vmem_limit_bytes=8 * 2**20),
        cost_estimate=cost(4 * rows * n, 2 * (4 + 3 * copies) * rows * n),
        name="column_sums",
    )(where, line)


def far_kernel(heads, slot, where_ref, got_ref, plane_ref, out_ref):
    group, rows, tok = out_ref.shape
    n = got_ref.shape[2]
    x = where_ref[0]
    local = {}
    for bit in range(3):
        for block in range(0, group, 2 << bit):
            parts = [got_ref[i, :rows] for i in siblings(block + (1 << bit), bit)]
            local[bit, block] = total_of(parts)
    shared = [total_of([plane_ref[i, 0] for i in siblings(x, bit)]) for bit in range(2)]
    for kind in (1, 2):
        shared.append(total_of([plane_ref[i, kind] for i in range(plane_ref.shape[0])]))
    for j in range(group):
        query = got_ref[j, rows : rows + tok]
        weights = jnp.concatenate(
            [
                got_ref[j, rows + tok + k * slot : rows + tok + (k + 1) * slot]
                for k in range(tok // n)
            ],
            axis=1,
        ).astype(f32)
        total = read_level(shared[0], query, weights, 3, heads)
        for level in range(1, 4):
            total = total + read_level(shared[level], query, weights, 3 + level, heads)
        for bit in range(3):
            if j >> bit & 1:
                block = j >> (bit + 1) << (bit + 1)
                total = total + read_level(local[bit, block], query, weights, bit, heads)
        out_ref[j] = total.astype(bf16)


def far_levels(where, got, plane, heads, slot, tok):
    group = got.shape[0]
    rows = plane.shape[2]
    vmem = pl.BlockSpec(memory_space=pltpu.VMEM)
    return pl.pallas_call(
        functools.partial(far_kernel, heads, slot),
        in_specs=[pl.BlockSpec(memory_space=pltpu.SMEM), vmem, vmem],
        out_specs=vmem,
        out_shape=jax.ShapeDtypeStruct((group, rows, tok), bf16),
        compiler_params=pltpu.CompilerParams(vmem_limit_bytes=VMEM_MIB * 2**20),
        cost_estimate=cost(12 * group * rows * tok * 128, 8 * group * rows * tok),
        name="far_levels",
    )(where, got, plane)


def project(where_ref, pieces, normed_ref, out_ref):
    mine = where_ref[1]
    half = normed_ref.shape[1]
    width = pieces[0].shape[1]
    for k in range(len(pieces) // 2):
        block = dot(pieces[2 * k][0], normed_ref[mine], NN)
        block = block + dot(pieces[2 * k + 1][0], normed_ref[1 - mine], NN)
        at = pl.multiple_of((where_ref[0] ^ k) * width, width)
        out_ref[:, pl.ds(at, width)] = block.T.astype(out_ref.dtype)


def finish_kernel(where_ref, *refs):
    pieces = refs[:8]
    acc_ref, silu_ref, far_ref, gain_ref, out_ref, normed_ref = refs[8:]

    @pl.when(pl.program_id(0) == 0)
    def _():
        rows = acc_ref.shape[0]
        gated = (acc_ref[...] + far_ref[...].astype(f32)) * silu_ref[...]
        squares = jnp.sum(gated * gated, axis=0, keepdims=True)
        scale = lax.rsqrt(squares / rows + epsilon)
        normed = (gated * scale * gain_ref[...]).astype(bf16)
        normed_ref[0] = normed[: rows // 2]
        normed_ref[1] = normed[rows // 2 :]

    project(where_ref, pieces, normed_ref, out_ref)


def keep_kernel(where_ref, *refs):
    project(where_ref, refs[:8], refs[8], refs[9])


def piece_specs(pieces, offset):
    _, cols, depth = pieces[0].shape
    return [
        pl.BlockSpec((1, cols, depth), lambda i, where: ((where[offset] + i) ^ where[4], 0, 0))
        for _ in pieces
    ]


def finish(where, pieces, acc, silu, far, gain):
    rows, tok = acc.shape
    z_size, cols, depth = pieces[0].shape
    steps = z_size // 2
    wide = cols * len(pieces) // 2

    def whole(array):
        return pl.BlockSpec(array.shape, lambda i, where: (0,) * array.ndim)

    others = [acc, silu, far, gain]
    return pl.pallas_call(
        finish_kernel,
        grid_spec=pltpu.PrefetchScalarGridSpec(
            num_scalar_prefetch=1,
            grid=(steps,),
            in_specs=piece_specs(pieces, 2) + [whole(a) for a in others],
            out_specs=[
                pl.BlockSpec((tok, wide), lambda i, where: (0, i)),
                pl.BlockSpec((2, rows // 2, tok), lambda i, where: (0, 0, 0)),
            ],
        ),
        out_shape=[
            jax.ShapeDtypeStruct((tok, wide * steps), bf16),
            jax.ShapeDtypeStruct((2, rows // 2, tok), bf16),
        ],
        compiler_params=params(40),
        cost_estimate=cost(2 * tok * rows * wide * steps, 16 * 2**20),
        name="finish",
    )(where, *pieces, *others)


def keep(where, pieces, normed):
    _, rows, tok = normed.shape
    z_size, cols, depth = pieces[0].shape
    steps = z_size // 2
    wide = cols * len(pieces) // 2
    return pl.pallas_call(
        keep_kernel,
        grid_spec=pltpu.PrefetchScalarGridSpec(
            num_scalar_prefetch=1,
            grid=(steps,),
            in_specs=piece_specs(pieces, 3)
            + [pl.BlockSpec((2, rows, tok), lambda i, where: (0, 0, 0))],
            out_specs=pl.BlockSpec((tok, wide), lambda i, where: (0, i)),
        ),
        out_shape=jax.ShapeDtypeStruct((tok, wide * steps), f32),
        compiler_params=params(40),
        cost_estimate=cost(2 * tok * 2 * rows * wide * steps, 8 * 2**20),
        name="keep",
    )(where, *pieces, normed)


def shared_along(value, axis):
    spread = jnp.broadcast_to(value[None], (lax.axis_size(axis), *value.shape))
    return lax.all_to_all(spread, axis, 0, 0, tiled=True)


def weight_line(out_weight):
    rows, cols = out_weight.shape
    mine = lax.axis_index("rep")
    half = lax.dynamic_slice_in_dim(out_weight, mine * (rows // 2), rows // 2, 0).T
    return shared_along(half, "y").reshape(-1, rows // 2)


def weight_pieces(halves):
    pieces = []
    for piece in halves:
        pieces += [piece, swapped(piece, "rep", 1)]
    return pieces


def on_device(
    seq_values, seq_gate, seq_keys, seq_queries, level_weights, skip_gain, norm_gain, out_weight
):
    tok, width = seq_values.shape
    n = seq_keys.shape[1]
    head_count = skip_gain.shape[0]
    head_size = width // head_count
    group = lax.axis_size("y")
    heads = head_count // group
    rows = width // group
    slot = 32
    axes = [("y", b) for b in range(3)] + [("x", b) for b in range(2)] + [("zl", b) for b in range(2)]
    uppers = jnp.stack([(lax.axis_index(a) >> b) & 1 for a, b in axes]).astype(f32)
    x, y, z, head = (lax.axis_index(a) for a in ("x", "y", "zl", "head"))
    z_half = lax.axis_size("zl") // 2
    place = jnp.stack([x, z]).astype(jnp.int32)
    where = jnp.stack(
        [x, lax.axis_index("rep"), (1 - head) * z_half, head * z_half, z]
    ).astype(jnp.int32)

    weight = weight_line(out_weight)
    vt, sent = to_group(uppers, seq_values, seq_keys, seq_queries, level_weights, group, slot)
    sent, weight = lax.optimization_barrier((sent, weight))
    raw = lax.all_to_all(sent, "y", 0, 0, tiled=True)
    planes = [swapped(weight, "zl", d) for d in range(1, lax.axis_size("zl"))]
    acc, silu = local_part(vt, seq_gate, seq_keys, seq_queries, level_weights, skip_gain, head_size)
    planes, acc, silu = lax.optimization_barrier((planes, acc, silu))
    own = jnp.stack([weight, *planes])
    near, last = swapped(own, "x", 1), swapped(own, "x", 3)
    raw, own = lax.optimization_barrier((raw, own))

    line = group_sum(raw, rows, lax.axis_size("zl"))
    line = lax.all_to_all(line, "zl", 0, 0, tiled=True)
    plane = column_sums(place, line, lax.axis_size("x"))
    plane = lax.all_to_all(plane, "x", 0, 0, tiled=True)
    plane, own, near, last = lax.optimization_barrier((plane, own, near, last))
    middle = swapped(own, "x", 2)
    pieces = weight_pieces([own, near, middle, last])
    far = far_levels(place, raw, plane, heads, slot, tok)
    far = lax.all_to_all(far, "y", 0, 0, tiled=True).reshape(width, tok)

    to_send, normed = finish(where, pieces, acc, silu, far, norm_gain[:, None])
    got = swapped(to_send, "head", 1)
    kept = keep(where, pieces, normed)
    return (kept + got.astype(f32)).astype(bf16)


def solution(mesh):
    grid = Mesh(mesh.devices.reshape(4, 4, 8, 2, 2), ("zl", "x", "y", "head", "rep"))
    ctx = ("zl", "x", "y")
    tokens = ("rep", *ctx)
    placed = (
        P(tokens, "head"),
        P(tokens, "head"),
        P(tokens, None),
        P(tokens, None),
        P(None, "head", tokens),
        P("head"),
        P("head"),
        P("head", ctx),
    )
    return jax.shard_map(
        on_device, mesh=grid, in_specs=placed, out_specs=P(tokens, "head"), check_vma=False
    )
```

```python
import functools

import jax
import jax.numpy as jnp
from jax import lax
from jax.experimental import pallas as pl
from jax.experimental.pallas import tpu as pltpu
from jax.sharding import Mesh, PartitionSpec as P

epsilon = 1e-05
LOCAL_LEVELS = 9
VMEM_MIB = 56
NN = (((1,), (0,)), ((), ()))
NT = (((1,), (1,)), ((), ()))
f32 = jnp.float32
bf16 = jnp.bfloat16


def params(mib, steps=1):
    return pltpu.CompilerParams(
        vmem_limit_bytes=mib * 2**20, dimension_semantics=("arbitrary",) * steps
    )


def cost(flops, moved):
    return pl.CostEstimate(flops=flops, bytes_accessed=moved, transcendentals=0)


def swapped(value, axis, mask):
    return lax.ppermute(value, axis, [(i, i ^ mask) for i in range(lax.axis_size(axis))])


def dot(a, b, dims):
    return lax.dot_general(a, b, dims, preferred_element_type=f32)


def send_kernel(heads, slot, upper_ref, values_ref, keys_ref, query_ref, w_ref, vt_ref, sent_ref):
    vt = values_ref[...].T
    vt_ref[...] = vt
    state = dot(vt, keys_ref[...], NN).astype(bf16)
    tok, n = query_ref.shape
    count = upper_ref.shape[0]
    shares = sent_ref.shape[0]
    rows = state.shape[0] // shares
    for e in range(shares):
        w = [
            w_ref[LOCAL_LEVELS + level, e * heads : (e + 1) * heads, :].astype(f32) * upper_ref[level]
            for level in range(count)
        ]
        w.append(jnp.zeros((slot - count * heads, tok), f32))
        w = jnp.concatenate(w, axis=0).astype(bf16)
        sent_ref[e, :rows] = state[e * rows : (e + 1) * rows]
        sent_ref[e, rows : rows + tok] = query_ref[...]
        for k in range(tok // n):
            first = rows + tok + k * slot
            sent_ref[e, first : first + slot] = w[:, k * n : (k + 1) * n]


def to_group(uppers, values, keys, query, weights, group, slot):
    tok, width = values.shape
    n = keys.shape[1]
    steps = 4
    cols = width // steps
    heads = weights.shape[1] // group
    rows = width // group + tok + tok // n * slot
    return pl.pallas_call(
        functools.partial(send_kernel, heads, slot),
        grid=(steps,),
        in_specs=[
            pl.BlockSpec(memory_space=pltpu.SMEM),
            pl.BlockSpec((tok, cols), lambda i: (0, i)),
            pl.BlockSpec((tok, n), lambda i: (0, 0)),
            pl.BlockSpec((tok, n), lambda i: (0, 0)),
            pl.BlockSpec((16, group // steps * heads, tok), lambda i: (0, i, 0)),
        ],
        out_specs=[
            pl.BlockSpec((cols, tok), lambda i: (i, 0)),
            pl.BlockSpec((group // steps, rows, n), lambda i: (i, 0, 0)),
        ],
        out_shape=[
            jax.ShapeDtypeStruct((width, tok), bf16),
            jax.ShapeDtypeStruct((group, rows, n), bf16),
        ],
        compiler_params=params(VMEM_MIB),
        cost_estimate=cost(2 * tok * width * n, 4 * tok * width),
        name="to_group",
    )(uppers, values, keys, query, weights)


def local_kernel(heads, half, skip_ref, vt_ref, gate_ref, keys_ref, query_ref, w_ref, acc_ref, silu_ref, score_ref):
    size = vt_ref.shape[0] // heads
    first = pl.program_id(0) * heads

    @pl.when(pl.program_id(0) == 0)
    def _():
        scores = dot(keys_ref[...], query_ref[...], NT)
        s = lax.broadcasted_iota(jnp.int32, scores.shape, 0)
        t = lax.broadcasted_iota(jnp.int32, scores.shape, 1)
        score_ref[...] = jnp.where(s <= t, scores, 0.0)

    gate = gate_ref[...].astype(f32)
    silu_ref[...] = (gate / (1.0 + jnp.exp(-gate))).T

    s = lax.broadcasted_iota(jnp.int32, (half, half), 0)
    t = lax.broadcasted_iota(jnp.int32, (half, half), 1)
    differ = s ^ t
    low = score_ref[:half, :half]
    cross = score_ref[:half, half:]
    high = score_ref[half:, half:]
    for h in range(heads):
        w = w_ref[:, h, :].astype(f32)

        def mix(level, lo):
            return jnp.broadcast_to(w[level : level + 1, lo : lo + half], (half, half))

        def diagonal(lo, scores):
            m = mix(0, lo)
            for level in range(1, LOCAL_LEVELS - 1):
                m = jnp.where(differ >= (1 << (level - 1)), mix(level, lo), m)
            return (m * scores).astype(bf16)

        vt = vt_ref[h * size : (h + 1) * size, :]
        skip = skip_ref[first + h]
        near = dot(vt[:, :half], diagonal(0, low), NN)
        right = jnp.concatenate(
            [(mix(LOCAL_LEVELS - 1, half) * cross).astype(bf16), diagonal(half, high)], axis=0
        )
        far = dot(vt, right, NN)
        rows = slice(h * size, (h + 1) * size)
        acc_ref[rows, :half] = near + skip * vt[:, :half].astype(f32)
        acc_ref[rows, half:] = far + skip * vt[:, half:].astype(f32)


def local_part(vt, gate, keys, query, weights, skip, head_size):
    cols, tok = vt.shape
    n = keys.shape[1]
    heads = 8
    rows = heads * head_size
    steps = cols // rows
    return pl.pallas_call(
        functools.partial(local_kernel, heads, tok // 2),
        grid=(steps,),
        in_specs=[
            pl.BlockSpec(memory_space=pltpu.SMEM),
            pl.BlockSpec((rows, tok), lambda i: (i, 0)),
            pl.BlockSpec((tok, rows), lambda i: (0, i)),
            pl.BlockSpec((tok, n), lambda i: (0, 0)),
            pl.BlockSpec((tok, n), lambda i: (0, 0)),
            pl.BlockSpec((16, heads, tok), lambda i: (0, i, 0)),
        ],
        out_specs=[
            pl.BlockSpec((rows, tok), lambda i: (i, 0)),
            pl.BlockSpec((rows, tok), lambda i: (i, 0)),
        ],
        out_shape=[jax.ShapeDtypeStruct((cols, tok), f32)] * 2,
        scratch_shapes=[pltpu.VMEM((tok, tok), f32)],
        compiler_params=params(VMEM_MIB),
        cost_estimate=cost(8 * tok * tok * cols, 12 * tok * cols),
        name="local_part",
    )(skip, vt, gate, keys, query, weights)


def read_level(state, query, weights, level, heads):
    rows, tok = state.shape[0], query.shape[0]
    part = dot(state, query, NT).reshape(heads, rows // heads, tok)
    return (part * weights[level * heads : (level + 1) * heads][:, None, :]).reshape(rows, tok)


def total_of(parts):
    total = parts[0].astype(f32)
    for part in parts[1:]:
        total = total + part.astype(f32)
    return total.astype(bf16)


def siblings(index, bit):
    first = ((index >> bit) ^ 1) << bit
    return [first + k for k in range(1 << bit)]


def group_kernel(got_ref, out_ref):
    total = total_of([got_ref[j] for j in range(got_ref.shape[0])])
    for k in range(out_ref.shape[0]):
        out_ref[k] = total


def group_sum(got, rows, copies):
    group, _, n = got.shape
    return pl.pallas_call(
        group_kernel,
        grid=(1,),
        in_specs=[pl.BlockSpec((group, rows, n), lambda i: (0, 0, 0))],
        out_specs=pl.BlockSpec((copies, rows, n), lambda i: (0, 0, 0)),
        out_shape=jax.ShapeDtypeStruct((copies, rows, n), bf16),
        compiler_params=params(8),
        cost_estimate=cost(group * rows * n, 2 * (group + copies) * rows * n),
        name="group_sum",
    )(got)


def column_kernel(where_ref, line_ref, out_ref):
    z = where_ref[1]
    sums = [line_ref[z]]
    sums += [total_of([line_ref[i] for i in siblings(z, bit)]) for bit in range(2)]
    for k in range(out_ref.shape[0]):
        for i, value in enumerate(sums):
            out_ref[k, i] = value


def column_sums(where, line, copies):
    _, rows, n = line.shape
    vmem = pl.BlockSpec(memory_space=pltpu.VMEM)
    return pl.pallas_call(
        column_kernel,
        in_specs=[pl.BlockSpec(memory_space=pltpu.SMEM), vmem],
        out_specs=vmem,
        out_shape=jax.ShapeDtypeStruct((copies, 3, rows, n), bf16),
        compiler_params=pltpu.CompilerParams(vmem_limit_bytes=8 * 2**20),
        cost_estimate=cost(4 * rows * n, 2 * (4 + 3 * copies) * rows * n),
        name="column_sums",
    )(where, line)


def far_kernel(heads, slot, where_ref, got_ref, plane_ref, out_ref):
    group, rows, tok = out_ref.shape
    n = got_ref.shape[2]
    x = where_ref[0]
    local = {}
    for bit in range(3):
        for block in range(0, group, 2 << bit):
            parts = [got_ref[i, :rows] for i in siblings(block + (1 << bit), bit)]
            local[bit, block] = total_of(parts)
    shared = [total_of([plane_ref[i, 0] for i in siblings(x, bit)]) for bit in range(2)]
    for kind in (1, 2):
        shared.append(total_of([plane_ref[i, kind] for i in range(plane_ref.shape[0])]))
    for j in range(group):
        query = got_ref[j, rows : rows + tok]
        weights = jnp.concatenate(
            [
                got_ref[j, rows + tok + k * slot : rows + tok + (k + 1) * slot]
                for k in range(tok // n)
            ],
            axis=1,
        ).astype(f32)
        total = read_level(shared[0], query, weights, 3, heads)
        for level in range(1, 4):
            total = total + read_level(shared[level], query, weights, 3 + level, heads)
        for bit in range(3):
            if j >> bit & 1:
                block = j >> (bit + 1) << (bit + 1)
                total = total + read_level(local[bit, block], query, weights, bit, heads)
        out_ref[j] = total.astype(bf16)


def far_levels(where, got, plane, heads, slot, tok):
    group = got.shape[0]
    rows = plane.shape[2]
    vmem = pl.BlockSpec(memory_space=pltpu.VMEM)
    return pl.pallas_call(
        functools.partial(far_kernel, heads, slot),
        in_specs=[pl.BlockSpec(memory_space=pltpu.SMEM), vmem, vmem],
        out_specs=vmem,
        out_shape=jax.ShapeDtypeStruct((group, rows, tok), bf16),
        compiler_params=pltpu.CompilerParams(vmem_limit_bytes=48 * 2**20),
        cost_estimate=cost(12 * group * rows * tok * 128, 8 * group * rows * tok),
        name="far_levels",
    )(where, got, plane)


def project(where_ref, pieces, normed_ref, out_ref):
    mine = where_ref[1]
    half = normed_ref.shape[1]
    width = pieces[0].shape[1]
    for k in range(len(pieces) // 2):
        block = dot(pieces[2 * k][0], normed_ref[mine], NN)
        block = block + dot(pieces[2 * k + 1][0], normed_ref[1 - mine], NN)
        at = pl.multiple_of((where_ref[0] ^ k) * width, width)
        out_ref[:, pl.ds(at, width)] = block.T.astype(out_ref.dtype)


def finish_kernel(where_ref, *refs):
    pieces = refs[:8]
    acc_ref, silu_ref, far_ref, gain_ref, out_ref, normed_ref = refs[8:]

    @pl.when(pl.program_id(0) == 0)
    def _():
        rows = acc_ref.shape[0]
        gated = (acc_ref[...] + far_ref[...].astype(f32)) * silu_ref[...]
        squares = jnp.sum(gated * gated, axis=0, keepdims=True)
        scale = lax.rsqrt(squares / rows + epsilon)
        normed = (gated * scale * gain_ref[...]).astype(bf16)
        normed_ref[0] = normed[: rows // 2]
        normed_ref[1] = normed[rows // 2 :]

    project(where_ref, pieces, normed_ref, out_ref)


def keep_kernel(where_ref, *refs):
    project(where_ref, refs[:8], refs[8], refs[9])


def piece_specs(pieces, offset):
    _, cols, depth = pieces[0].shape
    return [
        pl.BlockSpec((1, cols, depth), lambda i, where: ((where[offset] + i) ^ where[4], 0, 0))
        for _ in pieces
    ]


def finish(where, pieces, acc, silu, far, gain):
    rows, tok = acc.shape
    z_size, cols, depth = pieces[0].shape
    steps = z_size // 2
    wide = cols * len(pieces) // 2

    def whole(array):
        return pl.BlockSpec(array.shape, lambda i, where: (0,) * array.ndim)

    others = [acc, silu, far, gain]
    return pl.pallas_call(
        finish_kernel,
        grid_spec=pltpu.PrefetchScalarGridSpec(
            num_scalar_prefetch=1,
            grid=(steps,),
            in_specs=piece_specs(pieces, 2) + [whole(a) for a in others],
            out_specs=[
                pl.BlockSpec((tok, wide), lambda i, where: (0, i)),
                pl.BlockSpec((2, rows // 2, tok), lambda i, where: (0, 0, 0)),
            ],
        ),
        out_shape=[
            jax.ShapeDtypeStruct((tok, wide * steps), bf16),
            jax.ShapeDtypeStruct((2, rows // 2, tok), bf16),
        ],
        compiler_params=params(40),
        cost_estimate=cost(2 * tok * rows * wide * steps, 16 * 2**20),
        name="finish",
    )(where, *pieces, *others)


def keep(where, pieces, normed):
    _, rows, tok = normed.shape
    z_size, cols, depth = pieces[0].shape
    steps = z_size // 2
    wide = cols * len(pieces) // 2
    return pl.pallas_call(
        keep_kernel,
        grid_spec=pltpu.PrefetchScalarGridSpec(
            num_scalar_prefetch=1,
            grid=(steps,),
            in_specs=piece_specs(pieces, 3)
            + [pl.BlockSpec((2, rows, tok), lambda i, where: (0, 0, 0))],
            out_specs=pl.BlockSpec((tok, wide), lambda i, where: (0, i)),
        ),
        out_shape=jax.ShapeDtypeStruct((tok, wide * steps), f32),
        compiler_params=params(40),
        cost_estimate=cost(2 * tok * 2 * rows * wide * steps, 8 * 2**20),
        name="keep",
    )(where, *pieces, normed)


def shared_along(value, axis):
    spread = jnp.broadcast_to(value[None], (lax.axis_size(axis), *value.shape))
    return lax.all_to_all(spread, axis, 0, 0, tiled=True)


def weight_line(out_weight):
    rows, cols = out_weight.shape
    mine = lax.axis_index("rep")
    half = lax.dynamic_slice_in_dim(out_weight, mine * (rows // 2), rows // 2, 0).T
    return shared_along(half, "y").reshape(-1, rows // 2)


def weight_pieces(halves):
    pieces = []
    for piece in halves:
        pieces += [piece, swapped(piece, "rep", 1)]
    return pieces


def on_device(
    seq_values, seq_gate, seq_keys, seq_queries, level_weights, skip_gain, norm_gain, out_weight
):
    tok, width = seq_values.shape
    n = seq_keys.shape[1]
    head_count = skip_gain.shape[0]
    head_size = width // head_count
    group = lax.axis_size("y")
    heads = head_count // group
    rows = width // group
    slot = 32
    axes = [("y", b) for b in range(3)] + [("x", b) for b in range(2)] + [("zl", b) for b in range(2)]
    uppers = jnp.stack([(lax.axis_index(a) >> b) & 1 for a, b in axes]).astype(f32)
    x, y, z, head = (lax.axis_index(a) for a in ("x", "y", "zl", "head"))
    z_half = lax.axis_size("zl") // 2
    place = jnp.stack([x, z]).astype(jnp.int32)
    where = jnp.stack(
        [x, lax.axis_index("rep"), (1 - head) * z_half, head * z_half, z]
    ).astype(jnp.int32)

    weight = weight_line(out_weight)
    vt, sent = to_group(uppers, seq_values, seq_keys, seq_queries, level_weights, group, slot)
    sent, weight = lax.optimization_barrier((sent, weight))
    raw = lax.all_to_all(sent, "y", 0, 0, tiled=True)
    planes = [swapped(weight, "zl", d) for d in range(1, lax.axis_size("zl"))]
    acc, silu = local_part(vt, seq_gate, seq_keys, seq_queries, level_weights, skip_gain, head_size)
    planes, acc, silu = lax.optimization_barrier((planes, acc, silu))
    own = jnp.stack([weight, *planes])
    near, middle, last = [swapped(own, "x", k) for k in range(1, lax.axis_size("x"))]
    raw, own = lax.optimization_barrier((raw, own))

    line = group_sum(raw, rows, lax.axis_size("zl"))
    line = lax.all_to_all(line, "zl", 0, 0, tiled=True)
    plane = column_sums(place, line, lax.axis_size("x"))
    plane = lax.all_to_all(plane, "x", 0, 0, tiled=True)
    plane, own, near, last = lax.optimization_barrier((plane, own, near, last))
    pieces = weight_pieces([own, near, middle, last])
    far = far_levels(place, raw, plane, heads, slot, tok)
    far = lax.all_to_all(far, "y", 0, 0, tiled=True).reshape(width, tok)

    to_send, normed = finish(where, pieces, acc, silu, far, norm_gain[:, None])
    got = swapped(to_send, "head", 1)
    kept = keep(where, pieces, normed)
    return (kept + got.astype(f32)).astype(bf16)


def solution(mesh):
    grid = Mesh(mesh.devices.reshape(4, 4, 8, 2, 2), ("zl", "x", "y", "head", "rep"))
    ctx = ("zl", "x", "y")
    tokens = ("rep", *ctx)
    placed = (
        P(tokens, "head"),
        P(tokens, "head"),
        P(tokens, None),
        P(tokens, None),
        P(None, "head", tokens),
        P("head"),
        P("head"),
        P("head", ctx),
    )
    return jax.shard_map(
        on_device, mesh=grid, in_specs=placed, out_specs=P(tokens, "head"), check_vma=False
    )
```
